256 devices in a mesh: seq: 128 (over y, z, x), pipe: 2 (over core).
Axes of the slice: x: 4, y: 4, z: 8, core: 2. Of those that a mesh axis runs over, the one named last changes fastest.
Arguments:
- query_key: bfloat16 [2, 16384, 2048], P('pipe', 'seq'), may hold values from -6 to 6
- payload_matrix: bfloat16 [2, 16384, 2048], P('pipe', 'seq'), may hold values from -6 to 6
- out_grad: bfloat16 [2, 16384, 2048], P('pipe', 'seq'), may hold values from -6 to 6
- route_assignment: int32 [2, 128, 16], P('pipe'), may hold values from 0 to 63, as said below
Outputs:
- attn_out: bfloat16 [2, 16384, 2048], P('pipe', 'seq')
- grad_qk: bfloat16 [2, 16384, 2048], P('pipe', 'seq')
- grad_v: bfloat16 [2, 16384, 2048], P('pipe', 'seq')
The draws below stay inside these ranges and needn't reach their ends.
Inputs may be any that keep to these rules, and one draw needn't show every extreme that they name: `route_assignment`: in each section and head every cluster holds exactly 2 tiles. Cluster c of head h is owned by device 2 * c + (h mod 2) of seq. The 16 tile-head pairs of the tiles of one index of seq fall into clusters owned by one device at most 1 times, and exactly 1 times for some owner.
All inputs are finite; a program needn't handle non-finite values.
Results may differ from the reference program's by a relative error of at most 0.012.
The reference program's roundings to bfloat16 on the way count: a program that leaves them out, or rounds other values in their place, can miss the bound.
Values may be sent and summed in bfloat16 or wider, within the bound.
No kernel may reach another device: no remote copies, remote signals or barrier semaphores. Data moves between devices by JAX's collectives and lax.ppermute only.
A program may use at most 128 MiB of HBM per device.

```python
import jax
import jax.numpy as jnp
from jax import lax

HEADS = 16
HEAD_DIM = 128
TILE = 128
TILES_DEV = 1
D = 2048
TOKENS = 16384
TILES = 128
CLUSTERS = 64
MOST = 2
SECTIONS = 2
N_SEQ = 128


def draw_route_assignment(key, part):
    key = jax.random.fold_in(key, 3)
    table_list = []
    reader_roster = jnp.arange(HEADS, dtype=jnp.int32)
    tile_grid = jnp.arange(TILES_DEV, dtype=jnp.int32)
    spread = max(HEADS // 2, CLUSTERS // TILES_DEV)
    for section in range(SECTIONS):
        section_random_key = jax.random.fold_in(key, 500 + section)
        paired_keys = jax.random.split(section_random_key, 5)
        offsets = (jax.random.permutation(paired_keys[2], N_SEQ) // 2).astype(jnp.int32)
        order_rows = []
        for parity in range(2):
            order_key = jax.random.fold_in(paired_keys[4], parity)
            order_rows.append(jax.random.permutation(order_key, spread)[:HEADS // 2].astype(jnp.int32))
        orders = jnp.stack(order_rows)
        head_step = orders[reader_roster % 2, reader_roster // 2]
        shift_value = TILES_DEV * head_step[None, :] + tile_grid[:, None]
        cluster_labels = (offsets[:, None, None] + shift_value[None, :, :]) % CLUSTERS
        table_list.append(cluster_labels.reshape(TILES, HEADS))
    return jnp.stack(table_list).astype(jnp.int32)


def block_levels(rng, dims, pieces, least, high):
    gain, own = 1.0, jax.random.fold_in(rng, 6)
    for axis_at, blocks in pieces:
        draws = jnp.exp(jax.random.uniform(jax.random.fold_in(own, axis_at), (blocks,), jnp.float32, least / len(pieces), high / len(pieces)))
        gain = gain * jnp.repeat(draws, dims[axis_at] // blocks).reshape([-1 if axis == axis_at else 1 for axis in range(len(dims))])
    return gain


def centred(stream_key, shape, scale, limit, pieces=(), held_as=jnp.bfloat16):
    entries = scale * jax.random.normal(stream_key, shape, jnp.float32)
    if pieces:
        entries = entries * block_levels(stream_key, shape, pieces, -0.22, 0.18)
    return jnp.clip(entries, -limit, limit).astype(held_as)


def setup_inputs(seed: int = 0) -> dict:
    seeds = jax.random.split(jax.random.key(seed), 5)
    query_key = centred(seeds[0], (SECTIONS, TOKENS, D), 1.0, 6.0, ((0, 2), (1, 128)))
    payload_matrix = centred(seeds[1], (SECTIONS, TOKENS, D), 1.0, 6.0, ((0, 2), (1, 128)))
    out_grad = centred(seeds[2], (SECTIONS, TOKENS, D), 1.0, 6.0, ((0, 2), (1, 128)))
    route_assignment = draw_route_assignment(jax.random.fold_in(seeds[4], 71), 0)
    return {"query_key": query_key, "payload_matrix": payload_matrix, "out_grad": out_grad, "route_assignment": route_assignment}


logit_divisor_heat = 4.0
epsilon = 1e-06

def cluster_members(cluster_labels, cluster, most_tiles):
    hit_mask = cluster_labels == cluster
    rank_pos = jnp.cumsum(hit_mask.astype(jnp.int32)) - 1
    target = jnp.where(hit_mask, rank_pos, most_tiles).astype(jnp.int32)
    tile_ids = jnp.arange(cluster_labels.shape[0], dtype=jnp.int32)
    member_ids = jnp.zeros((most_tiles,), jnp.int32).at[target].set(tile_ids, mode='drop')
    member_count = jnp.sum(hit_mask.astype(jnp.int32))
    return (member_ids, jnp.arange(most_tiles, dtype=jnp.int32) < member_count)

def cluster_forward(common_lookup_vectors, values_in, positions, valid_rows):
    logit_multiplier = logit_divisor_heat / common_lookup_vectors.shape[-1]
    scores = jnp.dot(common_lookup_vectors, common_lookup_vectors.T, preferred_element_type=jnp.float32) * logit_multiplier
    allowed = valid_rows[None, :] & (positions[None, :] <= positions[:, None]) | jnp.eye(positions.shape[0], dtype=bool)
    weights = jnp.where(allowed, jnp.exp(scores), jnp.zeros_like(scores))
    attn_probs = (weights / lax.optimization_barrier(jnp.sum(weights, axis=1, keepdims=True))).astype(jnp.bfloat16)
    output = jnp.dot(attn_probs, values_in, preferred_element_type=jnp.float32).astype(jnp.bfloat16)
    return (output, attn_probs)

def cluster_backward(common_lookup_vectors, values_in, attn_probs, grad_rows, valid_rows):
    logit_multiplier = logit_divisor_heat / common_lookup_vectors.shape[-1]
    grad_rows = jnp.where(valid_rows[:, None], grad_rows, jnp.zeros_like(grad_rows))
    grad_probs = jnp.dot(grad_rows, values_in.T, preferred_element_type=jnp.float32)
    prob_values = attn_probs.astype(jnp.float32)
    row_total = lax.optimization_barrier(jnp.sum(prob_values * grad_probs, axis=1, keepdims=True))
    grad_scores = (prob_values * (grad_probs - row_total) * logit_multiplier).astype(jnp.bfloat16)
    grad_query = jnp.dot(grad_scores, common_lookup_vectors, preferred_element_type=jnp.float32)
    grad_query = grad_query + jnp.dot(grad_scores.T, common_lookup_vectors, preferred_element_type=jnp.float32)
    sensitivity_of_outputs = jnp.dot(attn_probs.T, grad_rows, preferred_element_type=jnp.float32)
    return (grad_query.astype(jnp.bfloat16), sensitivity_of_outputs.astype(jnp.bfloat16))

def head_pass(qk_head, value_head, grad_head, cluster_labels):
    raw_qk = qk_head.astype(jnp.float32)
    factor = lax.rsqrt(lax.optimization_barrier(jnp.mean(raw_qk * raw_qk, axis=-1, keepdims=True)) + epsilon)
    normed = (raw_qk * factor).astype(jnp.bfloat16)
    tile_offsets = jnp.arange(TILE, dtype=jnp.int32)

    def one_cluster(cluster):
        member_ids, member_valid = cluster_members(cluster_labels, cluster, MOST)
        positions = (member_ids[:, None] * TILE + tile_offsets[None, :]).reshape(-1)
        valid_rows = jnp.repeat(member_valid, TILE)
        output, attn_probs = cluster_forward(normed[positions], value_head[positions], positions, valid_rows)
        grad_query, sensitivity_of_outputs = cluster_backward(normed[positions], value_head[positions], attn_probs, grad_head[positions], valid_rows)
        targets = jnp.where(valid_rows, positions, TOKENS).astype(jnp.int32)
        return (output, grad_query, sensitivity_of_outputs, targets)
    outputs, query_gradient_rows, sensitivity_of_outputs, targets = lax.map(one_cluster, jnp.arange(CLUSTERS, dtype=jnp.int32))
    flat_targets = targets.reshape(-1)

    def spray_entries(grouped):
        empty = jnp.zeros((TOKENS, HEAD_DIM), grouped.dtype)
        return empty.at[flat_targets].set(grouped.reshape(-1, HEAD_DIM), mode='drop')
    attention = spray_entries(outputs)
    grad_normed = spray_entries(query_gradient_rows).astype(jnp.float32)
    grad_raw = factor * grad_normed - raw_qk * factor ** 3 * lax.optimization_barrier(jnp.mean(raw_qk * grad_normed, axis=-1, keepdims=True))
    return (attention, grad_raw.astype(jnp.bfloat16), spray_entries(sensitivity_of_outputs))

def section_pass(qk_rows, value_block, grad_block, cluster_labels):

    def per_head(head_id):
        start_col = (head_id * HEAD_DIM).astype(jnp.int32)
        qk_head = lax.dynamic_slice_in_dim(qk_rows, start_col, HEAD_DIM, 1)
        value_head = lax.dynamic_slice_in_dim(value_block, start_col, HEAD_DIM, 1)
        grad_head = lax.dynamic_slice_in_dim(grad_block, start_col, HEAD_DIM, 1)
        head_labels = lax.dynamic_index_in_dim(cluster_labels, head_id, 1, keepdims=False)
        return head_pass(qk_head, value_head, grad_head, head_labels)
    attention, grad_input, grad_value = lax.map(per_head, jnp.arange(HEADS, dtype=jnp.int32))

    def merge_heads(stacked):
        return jnp.transpose(stacked, (1, 0, 2)).reshape(TOKENS, HEADS * HEAD_DIM)
    return (merge_heads(attention), merge_heads(grad_input), merge_heads(grad_value))

def reference(query_key, payload_matrix, out_grad, route_assignment):
    attn_list = []
    grad_qk_list = []
    grad_v_list = []
    for section in range(SECTIONS):
        attention, grad_input, grad_value = section_pass(query_key[section], payload_matrix[section], out_grad[section], route_assignment[section])
        attn_list.append(attention)
        grad_qk_list.append(grad_input)
        grad_v_list.append(grad_value)
    attn_out = jnp.stack(attn_list)
    grad_qk = jnp.roll(jnp.stack(grad_qk_list), -1, axis=0)
    grad_v = jnp.roll(jnp.stack(grad_v_list), -1, axis=0)
    return (attn_out, grad_qk, grad_v)
```

```python
import jax
import jax.numpy as jnp
from jax import lax
from jax.experimental import pallas as pl
from jax.experimental.pallas import tpu as pltpu
from jax.sharding import PartitionSpec as P

HEADS = 16
HEAD_DIM = 128
TILE = 128
TILES = 128
SLICES = 8
ROWS = TILE // SLICES
MSG = 2 * ROWS + 8
STEP_HEADS = 4
STEPS = HEADS // STEP_HEADS
STEP_COLS = STEP_HEADS * HEAD_DIM
EPSILON = 1e-06
SCALE = 4.0 / HEAD_DIM
F32 = jnp.float32
BF16 = jnp.bfloat16


def dot_nt(a, b):
    return lax.dot_general(a, b, (((1,), (1,)), ((), ())), preferred_element_type=F32)


def dot_nn(a, b):
    return lax.dot_general(a, b, (((1,), (0,)), ((), ())), preferred_element_type=F32)


def dot_tn(a, b):
    return lax.dot_general(a, b, (((0,), (0,)), ((), ())), preferred_element_type=F32)


def split_pair(x):
    high = x.astype(BF16).astype(F32)
    return high, x - high


def normalise(raw):
    factor = lax.rsqrt(jnp.mean(raw * raw, axis=-1, keepdims=True) + EPSILON)
    return factor, (raw * factor).astype(BF16)


def head_columns(j):
    return slice(j * HEAD_DIM, (j + 1) * HEAD_DIM)


def pack_kernel(me_ref, route_ref, qk_hbm, v_hbm, g_hbm, o_ref, qk_buf, v_buf, g_buf, sems):
    inputs = ((qk_hbm, qk_buf), (v_hbm, v_buf), (g_hbm, g_buf))

    def copies(step):
        span = pl.ds(step * STEP_COLS, STEP_COLS)
        return [
            pltpu.make_async_copy(hbm.at[:, span], buf.at[:, span], sems.at[step, k])
            for k, (hbm, buf) in enumerate(inputs)
        ]

    for step in range(STEPS):
        for copy in copies(step):
            copy.start()

    me = me_ref[0]
    route = route_ref[...]
    own = route_ref[pl.ds(me, 1), :]
    tiles = lax.broadcasted_iota(jnp.int32, route.shape, 0)
    earlier = jnp.where((route == own) & (tiles < me), 1.0, 0.0)
    uppers = jnp.max(earlier, axis=0, keepdims=True)

    rows = lax.broadcasted_iota(jnp.int32, (TILE, TILE), 0)
    cols = lax.broadcasted_iota(jnp.int32, (TILE, TILE), 1)
    at_most = rows <= cols
    for j in range(HEADS):
        if j % STEP_HEADS == 0:
            for copy in copies(j // STEP_HEADS):
                copy.wait()
        upper = uppers[:, j : j + 1] > 0.0
        value = v_buf[:, head_columns(j)]
        grad = g_buf[:, head_columns(j)]
        _, normed = normalise(qk_buf[:, head_columns(j)].astype(F32))
        weights = jnp.where(at_most, jnp.exp(dot_nt(normed, normed) * SCALE), 0.0)
        grad_probs = dot_nt(value, grad)
        total = jnp.sum(weights, axis=0, keepdims=True)
        moment = jnp.sum(weights * grad_probs, axis=0, keepdims=True)
        stats = jnp.concatenate(
            [*split_pair(total), *split_pair(moment), jnp.zeros((4, TILE), F32)], axis=0
        ).astype(BF16)
        second = jnp.where(upper, grad.astype(F32), value.astype(F32)).astype(BF16)
        o_ref[j, :, 0:ROWS, :] = normed.reshape(SLICES, ROWS, HEAD_DIM)
        o_ref[j, :, ROWS : 2 * ROWS, :] = second.reshape(SLICES, ROWS, HEAD_DIM)
        o_ref[j, :, 2 * ROWS : MSG, :] = jnp.broadcast_to(
            stats[None], (SLICES, MSG - 2 * ROWS, TILE)
        )


def pack(me, route, qk, value, grad):
    buffer = pltpu.VMEM((TILE, HEADS * HEAD_DIM), BF16)
    hbm = pl.BlockSpec(memory_space=pltpu.HBM)
    whole = pl.BlockSpec(memory_space=pltpu.VMEM)
    return pl.pallas_call(
        pack_kernel,
        out_shape=jax.ShapeDtypeStruct((HEADS, SLICES, MSG, HEAD_DIM), BF16),
        in_specs=[pl.BlockSpec(memory_space=pltpu.SMEM), whole, hbm, hbm, hbm],
        out_specs=whole,
        scratch_shapes=[buffer, buffer, buffer, pltpu.SemaphoreType.DMA((STEPS, 3))],
        compiler_params=pltpu.CompilerParams(vmem_limit_bytes=16 * 1024 * 1024),
        name="pack",
    )(me, route, qk, value, grad)


def swap_kernel(partner_ref, x_ref, o_ref):
    def move(t, carry):
        o_ref[t] = x_ref[partner_ref[t]]
        return carry

    lax.fori_loop(0, TILES, move, 0, unroll=8)


def swap(partner, x):
    whole = pl.BlockSpec(memory_space=pltpu.VMEM)
    return pl.pallas_call(
        swap_kernel,
        out_shape=jax.ShapeDtypeStruct(x.shape, x.dtype),
        in_specs=[pl.BlockSpec(memory_space=pltpu.SMEM), whole],
        out_specs=whole,
        compiler_params=pltpu.CompilerParams(vmem_limit_bytes=16 * 1024 * 1024),
        name="swap",
    )(partner, x)


def finish_kernel(upper_ref, qk_ref, v_ref, g_ref, z_ref, out_ref, dqk_ref, dv_ref):
    rows = lax.broadcasted_iota(jnp.int32, (TILE, TILE), 0)
    cols = lax.broadcasted_iota(jnp.int32, (TILE, TILE), 1)
    causal = cols <= rows
    for j in range(HEADS):
        upper = upper_ref[j] != 0
        value = v_ref[:, head_columns(j)]
        grad = g_ref[:, head_columns(j)]
        raw = qk_ref[:, head_columns(j)].astype(F32)
        factor, normed = normalise(raw)
        second = jnp.where(upper, grad, value)
        their_normed = z_ref[j, :, 0:ROWS, :].reshape(TILE, HEAD_DIM)
        their_second = z_ref[j, :, ROWS : 2 * ROWS, :].reshape(TILE, HEAD_DIM)
        stats = z_ref[j, 0, 2 * ROWS : MSG, :].astype(F32)
        their_total = stats[0:1] + stats[1:2]
        their_moment = stats[2:3] + stats[3:4]

        weights = jnp.where(causal, jnp.exp(dot_nt(normed, normed) * SCALE), 0.0)
        cross = jnp.exp(dot_nt(normed, their_normed) * SCALE)
        grad_probs = dot_nt(grad, value)
        cross_grad_probs = dot_nt(second, their_second)

        row_total = jnp.sum(weights, axis=1, keepdims=True)
        cross_row = jnp.sum(cross, axis=1, keepdims=True)
        inv_row = 1.0 / (row_total + jnp.where(upper, cross_row, 0.0))
        inv_col = 1.0 / (their_total + jnp.sum(cross, axis=0, keepdims=True))
        probs = (weights * inv_row).astype(BF16)
        cross_probs = (cross * jnp.where(upper, inv_row, inv_col)).astype(BF16)
        probs_f = probs.astype(F32)
        cross_f = cross_probs.astype(F32)
        cross_terms = cross_f * cross_grad_probs
        row_sum = jnp.sum(probs_f * grad_probs, axis=1, keepdims=True)
        row_sum += jnp.where(upper, jnp.sum(cross_terms, axis=1, keepdims=True), 0.0)
        col_sum = their_moment * inv_col + jnp.sum(cross_terms, axis=0, keepdims=True)
        scores = (probs_f * (grad_probs - row_sum) * SCALE).astype(BF16)
        cross_scores = (
            cross_f * (cross_grad_probs - jnp.where(upper, row_sum, col_sum)) * SCALE
        ).astype(BF16)

        mixed = dot_nn(cross_probs, their_second)
        out = dot_nn(probs, value) + jnp.where(upper, mixed, 0.0)
        grad_value = dot_tn(probs, grad) + jnp.where(upper, 0.0, mixed)
        grad_normed = (
            dot_nn(scores, normed) + dot_tn(scores, normed) + dot_nn(cross_scores, their_normed)
        )
        grad_normed = grad_normed.astype(BF16).astype(F32)
        grad_input = factor * grad_normed - raw * factor**3 * jnp.mean(
            raw * grad_normed, axis=-1, keepdims=True
        )
        out_ref[:, head_columns(j)] = out.astype(BF16)
        dqk_ref[:, head_columns(j)] = grad_input.astype(BF16)
        dv_ref[:, head_columns(j)] = grad_value.astype(BF16)


def finish(upper, qk, value, grad, z):
    shape = jax.ShapeDtypeStruct((TILE, HEADS * HEAD_DIM), BF16)
    whole = pl.BlockSpec(memory_space=pltpu.VMEM)
    return pl.pallas_call(
        finish_kernel,
        out_shape=(shape, shape, shape),
        in_specs=[pl.BlockSpec(memory_space=pltpu.SMEM), whole, whole, whole, whole],
        out_specs=(whole, whole, whole),
        compiler_params=pltpu.CompilerParams(vmem_limit_bytes=16 * 1024 * 1024),
        name="finish",
    )(upper, qk, value, grad, z)


def exchange(x):
    return lax.all_to_all(x, "seq", split_axis=0, concat_axis=0, tiled=True)


def local(query_key, payload_matrix, out_grad, route_assignment):
    me = lax.axis_index("seq")
    route = route_assignment[0]
    tiles = jnp.arange(TILES, dtype=jnp.int32)

    own = lax.dynamic_index_in_dim(route, me, 0, keepdims=True)
    upper = jnp.any((route == own) & (tiles[:, None] < me), axis=0).astype(jnp.int32)

    labels = lax.dynamic_index_in_dim(route, me // SLICES, 1, keepdims=False)
    same = (labels[:, None] == labels[None, :]) & (tiles[:, None] != tiles[None, :])
    partner = jnp.sum(jnp.where(same, tiles[:, None], 0), axis=0)

    packed = pack(me.reshape(1), route, query_key[0], payload_matrix[0], out_grad[0])
    slices = exchange(packed.reshape(TILES, MSG, HEAD_DIM))
    swapped = swap(partner, slices)
    theirs = exchange(swapped).reshape(HEADS, SLICES, MSG, HEAD_DIM)
    out, grad_qk, grad_v = finish(upper, query_key[0], payload_matrix[0], out_grad[0], theirs)
    pairs = [(0, 1), (1, 0)]
    grad_qk, grad_v = lax.ppermute((grad_qk, grad_v), "pipe", pairs)
    return (out[None], grad_qk[None], grad_v[None])


def solution(mesh):
    rows = P("pipe", "seq", None)
    return jax.shard_map(
        local,
        mesh=mesh,
        in_specs=(rows, rows, rows, P("pipe", None, None)),
        out_specs=(rows, rows, rows),
        check_vma=False,
    )
```

```python
import jax
import jax.numpy as jnp
from jax import lax
from jax.experimental import pallas as pl
from jax.experimental.pallas import tpu as pltpu
from jax.sharding import PartitionSpec as P

HEADS = 16
HEAD_DIM = 128
TILE = 128
TILES = 128
SLICES = 8
PAIRS = TILE // SLICES // 2
MSG = 2 * PAIRS + 1
STEP_HEADS = 4
SWAP_STEPS = 4
STEPS = HEADS // STEP_HEADS
STEP_COLS = STEP_HEADS * HEAD_DIM
EPSILON = 1e-06
SCALE = 4.0 / HEAD_DIM
F32 = jnp.float32
BF16 = jnp.bfloat16
GROUP = 8
VMEM_LIMIT = 16 * 1024 * 1024


def dot_nt(a, b):
    return lax.dot_general(a, b, (((1,), (1,)), ((), ())), preferred_element_type=F32)


def dot_nn(a, b):
    return lax.dot_general(a, b, (((1,), (0,)), ((), ())), preferred_element_type=F32)


def dot_tn(a, b):
    return lax.dot_general(a, b, (((0,), (0,)), ((), ())), preferred_element_type=F32)


def split_pair(x):
    high = x.astype(BF16).astype(F32)
    return high, x - high


def normalise(raw):
    factor = lax.rsqrt(jnp.mean(raw * raw, axis=-1, keepdims=True) + EPSILON)
    return factor, (raw * factor).astype(BF16)


def head_columns(j):
    return slice(j * HEAD_DIM, (j + 1) * HEAD_DIM)


def grid_of(axis):
    return lax.broadcasted_iota(jnp.int32, (TILE, TILE), axis)


def pick(upper, if_upper, if_lower):
    return jnp.where(upper, if_upper.astype(F32), if_lower.astype(F32)).astype(BF16)


def in_step(heads):
    while heads:
        heads = [head for head in heads if next(head, head) is not head]


def pack_kernel(me_ref, route_hbm, qk_hbm, v_hbm, g_hbm, o_hbm, route_buf, o_buf, *scratch):
    buffers, sems = scratch[:3], scratch[3]
    inputs = (qk_hbm, v_hbm, g_hbm)

    def loads(step):
        span = pl.ds(step * STEP_COLS, STEP_COLS)
        return [
            pltpu.make_async_copy(hbm.at[:, span], buf.at[:, span], sems.at[step, k])
            for k, (hbm, buf) in enumerate(zip(inputs, buffers))
        ]

    def store(step):
        span = pl.ds(step * STEP_HEADS, STEP_HEADS)
        return pltpu.make_async_copy(o_buf.at[span], o_hbm.at[span], sems.at[step, 3])

    route_load = pltpu.make_async_copy(route_hbm, route_buf, sems.at[STEPS, 0])
    route_load.start()
    for step in range(STEPS):
        for load in loads(step):
            load.start()
    qk_buf, v_buf, g_buf = buffers

    route_load.wait()
    me = me_ref[0]
    route = route_buf[...]
    tiles = lax.broadcasted_iota(jnp.int32, route.shape, 1)
    own = jnp.sum(jnp.where(tiles == me, route, 0), axis=1, keepdims=True)
    earlier = jnp.where((route == own) & (tiles < me), 1.0, 0.0)
    uppers = jnp.max(earlier, axis=1, keepdims=True)
    at_most = grid_of(0) <= grid_of(1)

    def head(j):
        upper = uppers[j : j + 1, :] > 0.0
        value = v_buf[:, head_columns(j)]
        grad = g_buf[:, head_columns(j)]
        _, normed = normalise(qk_buf[:, head_columns(j)].astype(F32))
        second = pick(upper, grad, value)
        o_buf[j, :, 0:PAIRS] = normed.reshape(SLICES, PAIRS, 2, HEAD_DIM)
        o_buf[j, :, PAIRS : 2 * PAIRS] = second.reshape(SLICES, PAIRS, 2, HEAD_DIM)
        yield
        weights = jnp.where(at_most, jnp.exp(dot_nt(normed, normed) * SCALE), 0.0)
        grad_probs = dot_nt(value, grad)
        yield
        total = jnp.sum(weights, axis=0, keepdims=True)
        moment = jnp.sum(weights * grad_probs, axis=0, keepdims=True)
        yield
        stats = jnp.concatenate(
            [*split_pair(total), *split_pair(moment), jnp.zeros((12, TILE), F32)], axis=0
        ).astype(BF16)
        o_buf[j, :, 2 * PAIRS] = stats.reshape(SLICES, 2, TILE)

    for step in range(STEPS):
        for load in loads(step):
            load.wait()
        in_step([head(step * STEP_HEADS + j) for j in range(STEP_HEADS)])
        store(step).start()
    for step in range(STEPS):
        store(step).wait()


def pack(me, route, qk, value, grad):
    shape = (HEADS, SLICES, MSG, 2, HEAD_DIM)
    buffer = pltpu.VMEM((TILE, HEADS * HEAD_DIM), BF16)
    hbm = pl.BlockSpec(memory_space=pltpu.HBM)
    return pl.pallas_call(
        pack_kernel,
        out_shape=pltpu.HBM(shape, BF16),
        in_specs=[pl.BlockSpec(memory_space=pltpu.SMEM), hbm, hbm, hbm, hbm],
        out_specs=hbm,
        scratch_shapes=[
            pltpu.VMEM((HEADS, TILES), jnp.int32),
            pltpu.VMEM(shape, BF16),
            buffer,
            buffer,
            buffer,
            pltpu.SemaphoreType.DMA((STEPS + 1, 4)),
        ],
        compiler_params=pltpu.CompilerParams(vmem_limit_bytes=VMEM_LIMIT),
        name="pack",
    )(me, *[pltpu.with_memory_space_constraint(x, pltpu.HBM) for x in (route, qk, value, grad)])


def swap_kernel(partner_ref, x_ref, o_hbm, o_buf, sems):
    count = TILES // SWAP_STEPS

    def store(step):
        span = pl.ds(step * count, count)
        return pltpu.make_async_copy(o_buf.at[span], o_hbm.at[span], sems.at[step])

    def move(t, carry):
        o_buf[t] = x_ref[partner_ref[t]]
        return carry

    for step in range(SWAP_STEPS):
        lax.fori_loop(step * count, (step + 1) * count, move, 0, unroll=16)
        store(step).start()
    for step in range(SWAP_STEPS):
        store(step).wait()


def swap(partner, x):
    return pl.pallas_call(
        swap_kernel,
        out_shape=pltpu.HBM(x.shape, x.dtype),
        in_specs=[
            pl.BlockSpec(memory_space=pltpu.SMEM),
            pl.BlockSpec(memory_space=pltpu.VMEM),
        ],
        out_specs=pl.BlockSpec(memory_space=pltpu.HBM),
        scratch_shapes=[pltpu.VMEM(x.shape, x.dtype), pltpu.SemaphoreType.DMA((SWAP_STEPS,))],
        compiler_params=pltpu.CompilerParams(vmem_limit_bytes=VMEM_LIMIT),
        name="swap",
    )(partner, x)


def attend_kernel(
    upper_ref, qk_ref, v_ref, g_ref, z_ref, out_hbm, dv_ref, scores_ref, out_buf, sems
):
    def store(step):
        span = pl.ds(step * STEP_COLS, STEP_COLS)
        return pltpu.make_async_copy(out_buf.at[:, span], out_hbm.at[:, span], sems.at[step])

    ahead = grid_of(0) - grid_of(1)

    def head(j):
        upper = upper_ref[j] != 0
        value = v_ref[:, head_columns(j)]
        grad = g_ref[:, head_columns(j)]
        _, normed = normalise(qk_ref[:, head_columns(j)].astype(F32))
        second = pick(upper, grad, value)
        first = pick(upper, value, grad)
        their_normed = z_ref[j, :, 0:PAIRS].reshape(TILE, HEAD_DIM)
        their_second = z_ref[j, :, PAIRS : 2 * PAIRS].reshape(TILE, HEAD_DIM)
        stats = z_ref[j, :, 2 * PAIRS].reshape(2 * SLICES, TILE).astype(F32)
        their_total = stats[0:1] + stats[1:2]
        their_moment = stats[2:3] + stats[3:4]
        keys = jnp.concatenate([normed, their_normed], axis=0)
        others = jnp.concatenate([first, their_second], axis=0)
        yield
        weights = jnp.exp(dot_nt(normed, keys) * SCALE)
        grad_probs = dot_nt(second, others)
        yield
        inside = jnp.where(upper, ahead, -ahead) >= 0
        own_w = jnp.where(inside, weights[:, :TILE], 0.0)
        cross_w = weights[:, TILE:]
        own_g = grad_probs[:, :TILE]
        cross_g = grad_probs[:, TILE:]
        inv_row = 1.0 / jnp.sum(own_w + cross_w, axis=1, keepdims=True)
        own_inv = 1.0 / jnp.sum(own_w, axis=0, keepdims=True)
        cross_inv = 1.0 / (their_total + jnp.sum(cross_w, axis=0, keepdims=True))
        yield
        own_p = (own_w * jnp.where(upper, inv_row, own_inv)).astype(BF16)
        cross_p = (cross_w * jnp.where(upper, inv_row, cross_inv)).astype(BF16)
        own_f = own_p.astype(F32)
        cross_f = cross_p.astype(F32)
        own_t = own_f * own_g
        cross_t = cross_f * cross_g
        yield
        row_sum = jnp.sum(own_t + cross_t, axis=1, keepdims=True)
        own_sum = jnp.sum(own_t, axis=0, keepdims=True)
        cross_sum = their_moment * cross_inv + jnp.sum(cross_t, axis=0, keepdims=True)
        yield
        own_s = own_f * (own_g - jnp.where(upper, row_sum, own_sum)) * SCALE
        cross_s = cross_f * (cross_g - jnp.where(upper, row_sum, cross_sum)) * SCALE
        scores_ref[j, :, :TILE] = own_s.astype(BF16)
        scores_ref[j, :, TILE:] = cross_s.astype(BF16)
        along = dot_nn(jnp.concatenate([own_p, cross_p], axis=1), others)
        across = dot_tn(own_p, second)
        yield
        out_buf[:, head_columns(j)] = jnp.where(upper, along, across).astype(BF16)
        dv_ref[:, head_columns(j)] = jnp.where(upper, across, along).astype(BF16)

    for start in range(0, HEADS, GROUP):
        in_step([head(start + j) for j in range(GROUP)])
        for step in range(start // STEP_HEADS, (start + GROUP) // STEP_HEADS):
            store(step).start()
    for step in range(STEPS):
        store(step).wait()


def attend(upper, qk, value, grad, z):
    shape = jax.ShapeDtypeStruct((TILE, HEADS * HEAD_DIM), BF16)
    scores = jax.ShapeDtypeStruct((HEADS, TILE, 2 * TILE), BF16)
    whole = pl.BlockSpec(memory_space=pltpu.VMEM)
    return pl.pallas_call(
        attend_kernel,
        out_shape=(pltpu.HBM(shape.shape, shape.dtype), shape, scores),
        in_specs=[pl.BlockSpec(memory_space=pltpu.SMEM)] + [whole] * 4,
        out_specs=(pl.BlockSpec(memory_space=pltpu.HBM), whole, whole),
        scratch_shapes=[pltpu.VMEM(shape.shape, BF16), pltpu.SemaphoreType.DMA((STEPS,))],
        compiler_params=pltpu.CompilerParams(vmem_limit_bytes=VMEM_LIMIT),
        name="attend",
    )(upper, qk, value, grad, z)


def input_grad_kernel(qk_ref, z_ref, scores_ref, dqk_ref):
    def head(j):
        raw = qk_ref[:, head_columns(j)].astype(F32)
        factor, normed = normalise(raw)
        their_normed = z_ref[j, :, 0:PAIRS].reshape(TILE, HEAD_DIM)
        keys = jnp.concatenate([normed, their_normed], axis=0)
        yield
        grad_normed = dot_nn(scores_ref[j], keys) + dot_tn(scores_ref[j, :, :TILE], normed)
        grad_normed = grad_normed.astype(BF16).astype(F32)
        yield
        inner = jnp.mean(raw * grad_normed, axis=-1, keepdims=True)
        grad_input = factor * grad_normed - raw * (factor**3 * inner)
        dqk_ref[:, head_columns(j)] = grad_input.astype(BF16)

    for start in range(0, HEADS, GROUP):
        in_step([head(start + j) for j in range(GROUP)])


def input_grad(qk, z, scores):
    whole = pl.BlockSpec(memory_space=pltpu.VMEM)
    return pl.pallas_call(
        input_grad_kernel,
        out_shape=jax.ShapeDtypeStruct((TILE, HEADS * HEAD_DIM), BF16),
        in_specs=[whole] * 3,
        out_specs=whole,
        compiler_params=pltpu.CompilerParams(vmem_limit_bytes=VMEM_LIMIT),
        cost_estimate=pl.CostEstimate(
            flops=HEADS * 6 * TILE * TILE * HEAD_DIM, bytes_accessed=3 * 1024 * 1024, transcendentals=0
        ),
        name="input_grad",
    )(qk, z, scores)


def exchange(x):
    return lax.all_to_all(x, "seq", split_axis=0, concat_axis=0, tiled=True)


def local(query_key, payload_matrix, out_grad, route_assignment):
    me = lax.axis_index("seq")
    route = route_assignment[0]
    rows = (query_key[0], payload_matrix[0], out_grad[0])
    tiles = jnp.arange(TILES, dtype=jnp.int32)

    own = lax.dynamic_index_in_dim(route, me, 0, keepdims=True)
    upper = jnp.any((route == own) & (tiles[:, None] < me), axis=0).astype(jnp.int32)

    labels = lax.dynamic_index_in_dim(route, me // SLICES, 1, keepdims=False)
    same = (labels[:, None] == labels[None, :]) & (tiles[:, None] != tiles[None, :])
    partner = jnp.sum(jnp.where(same, tiles[:, None], 0), axis=0)

    packed = pack(me.reshape(1), route.T, *rows)
    slices = exchange(packed.reshape(TILES, MSG, 2, HEAD_DIM))
    theirs = exchange(swap(partner, slices)).reshape(HEADS, SLICES, MSG, 2, HEAD_DIM)
    out, grad_v, scores = attend(upper, *rows, theirs)
    pairs = [(0, 1), (1, 0)]
    grad_v = lax.ppermute(grad_v, "pipe", pairs)
    grad_qk = lax.ppermute(input_grad(rows[0], theirs, scores), "pipe", pairs)
    return (out[None], grad_qk[None], grad_v[None])


def solution(mesh):
    rows = P("pipe", "seq", None)
    return jax.shard_map(
        local,
        mesh=mesh,
        in_specs=(rows, rows, rows, P("pipe", None, None)),
        out_specs=(rows, rows, rows),
        check_vma=False,
    )
```

```python
import math

import jax
import jax.numpy as jnp
from jax import lax
from jax.experimental import pallas as pl
from jax.experimental.pallas import tpu as pltpu
from jax.sharding import PartitionSpec as P

HEADS = 16
HEAD_DIM = 128
TILE = 128
TILES = 128
SLICES = 8
PAIRS = TILE // SLICES // 2
MSG = 2 * PAIRS + 1
STEP_HEADS = 4
STEPS = HEADS // STEP_HEADS
STEP_COLS = STEP_HEADS * HEAD_DIM
EPSILON = 1e-06
SCALE = 4.0 / HEAD_DIM
SCALE_LOG2 = SCALE * math.log2(math.e)
F32 = jnp.float32
BF16 = jnp.bfloat16
GROUP = 8
VMEM_LIMIT = 16 * 1024 * 1024


def dot_nt(a, b):
    return lax.dot_general(a, b, (((1,), (1,)), ((), ())), preferred_element_type=F32)


def dot_nn(a, b):
    return lax.dot_general(a, b, (((1,), (0,)), ((), ())), preferred_element_type=F32)


def dot_tn(a, b):
    return lax.dot_general(a, b, (((0,), (0,)), ((), ())), preferred_element_type=F32)


def split_pair(x):
    high = x.astype(BF16).astype(F32)
    return high, x - high


def normalise(raw):
    factor = lax.rsqrt(jnp.mean(raw * raw, axis=-1, keepdims=True) + EPSILON)
    return factor, (raw * factor).astype(BF16)


def head_columns(j):
    return slice(j * HEAD_DIM, (j + 1) * HEAD_DIM)


def grid_of(axis):
    return lax.broadcasted_iota(jnp.int32, (TILE, TILE), axis)


def pick(upper, if_upper, if_lower):
    return jnp.where(upper, if_upper.astype(F32), if_lower.astype(F32)).astype(BF16)


def in_step(heads):
    while heads:
        heads = [head for head in heads if next(head, head) is not head]


def pack_kernel(
    me_ref, route_hbm, qk_hbm, v_hbm, g_hbm, o_ref, upper_ref, partner_ref, route_buf, *scratch
):
    buffers, sems = scratch[:3], scratch[3]
    inputs = (qk_hbm, v_hbm, g_hbm)

    def loads(step):
        span = pl.ds(step * STEP_COLS, STEP_COLS)
        return [
            pltpu.make_async_copy(hbm.at[:, span], buf.at[:, span], sems.at[step, k])
            for k, (hbm, buf) in enumerate(zip(inputs, buffers))
        ]

    route_load = pltpu.make_async_copy(route_hbm, route_buf, sems.at[STEPS, 0])
    route_load.start()
    for step in range(STEPS):
        for load in loads(step):
            load.start()
    qk_buf, v_buf, g_buf = buffers

    route_load.wait()
    me = me_ref[0]
    route = route_buf[...]
    tiles = lax.broadcasted_iota(jnp.int32, route.shape, 1)
    own = jnp.sum(jnp.where(tiles == me, route, 0), axis=1, keepdims=True)
    earlier = jnp.where((route == own) & (tiles < me), 1.0, 0.0)
    uppers = jnp.max(earlier, axis=1, keepdims=True)
    upper_ref[...] = uppers.astype(jnp.int32)
    heads = lax.broadcasted_iota(jnp.int32, route.shape, 0)
    labels = jnp.sum(jnp.where(heads == me // SLICES, route, 0), axis=0, keepdims=True)
    labels = jnp.broadcast_to(labels, (TILES, TILES))
    diagonal = grid_of(0) == grid_of(1)
    column = jnp.sum(jnp.where(diagonal, labels, 0), axis=1, keepdims=True)
    same = (labels == column) & jnp.logical_not(diagonal)
    partner_ref[...] = jnp.sum(jnp.where(same, grid_of(0), 0), axis=0, keepdims=True)
    at_most = grid_of(0) <= grid_of(1)

    def head(j):
        upper = uppers[j : j + 1, :] > 0.0
        value = v_buf[:, head_columns(j)]
        grad = g_buf[:, head_columns(j)]
        _, normed = normalise(qk_buf[:, head_columns(j)].astype(F32))
        second = pick(upper, grad, value)
        o_ref[j, :, 0:PAIRS] = normed.reshape(SLICES, PAIRS, 2, HEAD_DIM)
        o_ref[j, :, PAIRS : 2 * PAIRS] = second.reshape(SLICES, PAIRS, 2, HEAD_DIM)
        yield
        weights = jnp.where(at_most, jnp.exp2(dot_nt(normed, normed) * SCALE_LOG2), 0.0)
        grad_probs = dot_nt(value, grad)
        yield
        total = jnp.sum(weights, axis=0, keepdims=True)
        moment = jnp.sum(weights * grad_probs, axis=0, keepdims=True)
        yield
        stats = jnp.concatenate(
            [*split_pair(total), *split_pair(moment), jnp.zeros((12, TILE), F32)], axis=0
        ).astype(BF16)
        o_ref[j, :, 2 * PAIRS] = stats.reshape(SLICES, 2, TILE)

    for step in range(STEPS):
        for load in loads(step):
            load.wait()
        in_step([head(step * STEP_HEADS + j) for j in range(STEP_HEADS)])


def pack(me, route, qk, value, grad):
    shape = (HEADS, SLICES, MSG, 2, HEAD_DIM)
    buffer = pltpu.VMEM((TILE, HEADS * HEAD_DIM), BF16)
    hbm = pl.BlockSpec(memory_space=pltpu.HBM)
    return pl.pallas_call(
        pack_kernel,
        out_shape=(
            jax.ShapeDtypeStruct(shape, BF16),
            jax.ShapeDtypeStruct((HEADS, 1), jnp.int32),
            jax.ShapeDtypeStruct((1, TILES), jnp.int32),
        ),
        in_specs=[pl.BlockSpec(memory_space=pltpu.SMEM), hbm, hbm, hbm, hbm],
        out_specs=(pl.BlockSpec(memory_space=pltpu.VMEM),) * 3,
        scratch_shapes=[
            pltpu.VMEM((HEADS, TILES), jnp.int32),
            buffer,
            buffer,
            buffer,
            pltpu.SemaphoreType.DMA((STEPS + 1, 3)),
        ],
        compiler_params=pltpu.CompilerParams(vmem_limit_bytes=VMEM_LIMIT),
        name="pack",
    )(me, *[pltpu.with_memory_space_constraint(x, pltpu.HBM) for x in (route, qk, value, grad)])


def swap_kernel(partner_ref, x_ref, o_ref):
    def move(t, carry):
        o_ref[t] = x_ref[partner_ref[0, t]]
        return carry

    lax.fori_loop(0, TILES, move, 0, unroll=16)


def swap(partner, x):
    whole = pl.BlockSpec(memory_space=pltpu.VMEM)
    return pl.pallas_call(
        swap_kernel,
        out_shape=jax.ShapeDtypeStruct(x.shape, x.dtype),
        in_specs=[pl.BlockSpec(memory_space=pltpu.SMEM), whole],
        out_specs=whole,
        compiler_params=pltpu.CompilerParams(vmem_limit_bytes=VMEM_LIMIT),
        name="swap",
    )(partner, x)


def finish_kernel(
    upper_ref, qk_ref, v_ref, g_ref, z_ref, out_hbm, dqk_ref, dv_ref, out_buf, sems
):
    def store(step):
        span = pl.ds(step * STEP_COLS, STEP_COLS)
        return pltpu.make_async_copy(out_buf.at[:, span], out_hbm.at[:, span], sems.at[step])

    ahead = grid_of(0) - grid_of(1)

    def head(j):
        upper = upper_ref[j, 0] != 0
        value = v_ref[:, head_columns(j)]
        grad = g_ref[:, head_columns(j)]
        raw = qk_ref[:, head_columns(j)].astype(F32)
        factor, normed = normalise(raw)
        second = pick(upper, grad, value)
        first = pick(upper, value, grad)
        their_normed = z_ref[j, :, 0:PAIRS].reshape(TILE, HEAD_DIM)
        their_second = z_ref[j, :, PAIRS : 2 * PAIRS].reshape(TILE, HEAD_DIM)
        stats = z_ref[j, :, 2 * PAIRS].reshape(2 * SLICES, TILE).astype(F32)
        their_total = stats[0:1] + stats[1:2]
        their_moment = stats[2:3] + stats[3:4]
        keys = jnp.concatenate([normed, their_normed], axis=0)
        others = jnp.concatenate([first, their_second], axis=0)
        yield
        weights = jnp.exp2(dot_nt(normed, keys) * SCALE_LOG2)
        grad_probs = dot_nt(second, others)
        yield
        inside = jnp.where(upper, ahead, -ahead) >= 0
        own_w = jnp.where(inside, weights[:, :TILE], 0.0)
        cross_w = weights[:, TILE:]
        own_g = grad_probs[:, :TILE]
        cross_g = grad_probs[:, TILE:]
        inv_row = 1.0 / jnp.sum(own_w + cross_w, axis=1, keepdims=True)
        own_inv = 1.0 / jnp.sum(own_w, axis=0, keepdims=True)
        cross_inv = 1.0 / (their_total + jnp.sum(cross_w, axis=0, keepdims=True))
        yield
        own_p = (own_w * jnp.where(upper, inv_row, own_inv)).astype(BF16)
        cross_p = (cross_w * jnp.where(upper, inv_row, cross_inv)).astype(BF16)
        own_f = own_p.astype(F32)
        cross_f = cross_p.astype(F32)
        own_t = own_f * own_g
        cross_t = cross_f * cross_g
        yield
        row_sum = jnp.sum(own_t + cross_t, axis=1, keepdims=True)
        own_sum = jnp.sum(own_t, axis=0, keepdims=True)
        cross_sum = their_moment * cross_inv + jnp.sum(cross_t, axis=0, keepdims=True)
        yield
        own_s = own_f * (own_g - jnp.where(upper, row_sum, own_sum))
        cross_s = cross_f * (cross_g - jnp.where(upper, row_sum, cross_sum))
        own_s = own_s.astype(BF16)
        scores = jnp.concatenate([own_s, cross_s.astype(BF16)], axis=1)
        along = dot_nn(jnp.concatenate([own_p, cross_p], axis=1), others)
        across = dot_tn(own_p, second)
        grad_normed = dot_nn(scores, keys) + dot_tn(own_s, normed)
        yield
        out_buf[:, head_columns(j)] = jnp.where(upper, along, across).astype(BF16)
        dv_ref[:, head_columns(j)] = jnp.where(upper, across, along).astype(BF16)
        grad_normed = (grad_normed * SCALE).astype(BF16).astype(F32)
        inner = jnp.mean(raw * grad_normed, axis=-1, keepdims=True)
        grad_input = factor * grad_normed - raw * (factor**3 * inner)
        dqk_ref[:, head_columns(j)] = grad_input.astype(BF16)

    for start in range(0, HEADS, GROUP):
        in_step([head(start + j) for j in range(GROUP)])
        for step in range(start // STEP_HEADS, (start + GROUP) // STEP_HEADS):
            store(step).start()
    for step in range(STEPS):
        store(step).wait()


def finish(upper, qk, value, grad, z):
    shape = jax.ShapeDtypeStruct((TILE, HEADS * HEAD_DIM), BF16)
    whole = pl.BlockSpec(memory_space=pltpu.VMEM)
    return pl.pallas_call(
        finish_kernel,
        out_shape=(pltpu.HBM(shape.shape, shape.dtype), shape, shape),
        in_specs=[pl.BlockSpec(memory_space=pltpu.SMEM)] + [whole] * 4,
        out_specs=(pl.BlockSpec(memory_space=pltpu.HBM), whole, whole),
        scratch_shapes=[pltpu.VMEM(shape.shape, BF16), pltpu.SemaphoreType.DMA((STEPS,))],
        compiler_params=pltpu.CompilerParams(vmem_limit_bytes=VMEM_LIMIT),
        name="finish",
    )(upper, qk, value, grad, z)


def deliver_kernel(a_ref, b_ref, a_hbm, b_hbm, sems):
    copies = [
        pltpu.make_async_copy(a_ref, a_hbm, sems.at[0]),
        pltpu.make_async_copy(b_ref, b_hbm, sems.at[1]),
    ]
    for copy in copies:
        copy.start()
    for copy in copies:
        copy.wait()


def deliver(a, b):
    whole = pl.BlockSpec(memory_space=pltpu.VMEM)
    hbm = pl.BlockSpec(memory_space=pltpu.HBM)
    return pl.pallas_call(
        deliver_kernel,
        out_shape=(pltpu.HBM(a.shape, a.dtype), pltpu.HBM(b.shape, b.dtype)),
        in_specs=[whole, whole],
        out_specs=(hbm, hbm),
        scratch_shapes=[pltpu.SemaphoreType.DMA((2,))],
        compiler_params=pltpu.CompilerParams(vmem_limit_bytes=VMEM_LIMIT),
        name="deliver",
    )(a, b)


def exchange(x):
    return lax.all_to_all(x, "seq", split_axis=0, concat_axis=0, tiled=True)


def local(query_key, payload_matrix, out_grad, route_assignment):
    me = lax.axis_index("seq")
    route = route_assignment[0]
    rows = (query_key[0], payload_matrix[0], out_grad[0])
    packed, upper, partner = pack(me.reshape(1), route.T, *rows)
    slices = exchange(packed.reshape(TILES, MSG, 2, HEAD_DIM))
    theirs = exchange(swap(partner, slices)).reshape(HEADS, SLICES, MSG, 2, HEAD_DIM)
    out, grad_qk, grad_v = finish(upper, *rows, theirs)
    grad_qk, grad_v = deliver(*lax.ppermute((grad_qk, grad_v), "pipe", [(0, 1), (1, 0)]))
    return (out[None], grad_qk[None], grad_v[None])


def solution(mesh):
    rows = P("pipe", "seq", None)
    return jax.shard_map(
        local,
        mesh=mesh,
        in_specs=(rows, rows, rows, P("pipe", None, None)),
        out_specs=(rows, rows, rows),
        check_vma=False,
    )
```

```python
import math

import jax
import jax.numpy as jnp
from jax import lax
from jax.experimental import pallas as pl
from jax.experimental.pallas import tpu as pltpu
from jax.sharding import PartitionSpec as P

HEADS = 16
HEAD_DIM = 128
TILE = 128
TILES = 128
SLICES = 8
PAIRS = TILE // SLICES // 2
MSG = 2 * PAIRS + 1
STEP_HEADS = 4
STEPS = HEADS // STEP_HEADS
STEP_COLS = STEP_HEADS * HEAD_DIM
EPSILON = 1e-06
SCALE = 4.0 / HEAD_DIM
SCALE_LOG2 = SCALE * math.log2(math.e)
F32 = jnp.float32
BF16 = jnp.bfloat16
GROUP = 8
VMEM_LIMIT = 16 * 1024 * 1024


def dot_nt(a, b):
    return lax.dot_general(a, b, (((1,), (1,)), ((), ())), preferred_element_type=F32)


def dot_nn(a, b):
    return lax.dot_general(a, b, (((1,), (0,)), ((), ())), preferred_element_type=F32)


def dot_tn(a, b):
    return lax.dot_general(a, b, (((0,), (0,)), ((), ())), preferred_element_type=F32)


def split_pair(x):
    high = x.astype(BF16).astype(F32)
    return high, x - high


def normalise(raw):
    factor = lax.rsqrt(jnp.mean(raw * raw, axis=-1, keepdims=True) + EPSILON)
    return factor, (raw * factor).astype(BF16)


def head_columns(j):
    return slice(j * HEAD_DIM, (j + 1) * HEAD_DIM)


def grid_of(axis):
    return lax.broadcasted_iota(jnp.int32, (TILE, TILE), axis)


def pick(upper, if_upper, if_lower):
    return jnp.where(upper, if_upper, if_lower)


def in_step(heads):
    while heads:
        heads = [head for head in heads if next(head, head) is not head]


def pack_kernel(
    route_hbm, qk_hbm, v_hbm, g_hbm, o_ref, upper_ref, partner_ref, route_buf, *scratch
):
    buffers, sems = scratch[:3], scratch[3]
    inputs = (qk_hbm, v_hbm, g_hbm)

    def loads(step):
        span = pl.ds(step * STEP_COLS, STEP_COLS)
        return [
            pltpu.make_async_copy(hbm.at[:, span], buf.at[:, span], sems.at[step, k])
            for k, (hbm, buf) in enumerate(zip(inputs, buffers))
        ]

    route_load = pltpu.make_async_copy(route_hbm, route_buf, sems.at[STEPS, 0])
    route_load.start()
    for step in range(STEPS):
        for load in loads(step):
            load.start()
    qk_buf, v_buf, g_buf = buffers

    route_load.wait()
    me = lax.axis_index("seq")
    route = route_buf[...]
    tiles = lax.broadcasted_iota(jnp.int32, route.shape, 1)
    own = jnp.sum(jnp.where(tiles == me, route, 0), axis=1, keepdims=True)
    earlier = jnp.where((route == own) & (tiles < me), 1.0, 0.0)
    uppers = jnp.max(earlier, axis=1, keepdims=True)
    upper_ref[...] = uppers.astype(jnp.int32)
    heads = lax.broadcasted_iota(jnp.int32, route.shape, 0)
    labels = jnp.sum(jnp.where(heads == me // SLICES, route, 0), axis=0, keepdims=True)
    labels = jnp.broadcast_to(labels, (TILES, TILES))
    diagonal = grid_of(0) == grid_of(1)
    column = jnp.sum(jnp.where(diagonal, labels, 0), axis=1, keepdims=True)
    same = (labels == column) & jnp.logical_not(diagonal)
    partner_ref[...] = jnp.sum(jnp.where(same, grid_of(0), 0), axis=0, keepdims=True)
    at_most = grid_of(0) <= grid_of(1)

    def head(j):
        upper = uppers[j : j + 1, :] > 0.0
        value = v_buf[:, head_columns(j)]
        grad = g_buf[:, head_columns(j)]
        _, normed = normalise(qk_buf[:, head_columns(j)].astype(F32))
        second = pick(upper, grad, value)
        o_ref[j, :, 0:PAIRS] = normed.reshape(SLICES, PAIRS, 2, HEAD_DIM)
        o_ref[j, :, PAIRS : 2 * PAIRS] = second.reshape(SLICES, PAIRS, 2, HEAD_DIM)
        yield
        weights = jnp.where(at_most, jnp.exp2(dot_nt(normed, normed) * SCALE_LOG2), 0.0)
        grad_probs = dot_nt(value, grad)
        yield
        total = jnp.sum(weights, axis=0, keepdims=True)
        moment = jnp.sum(weights * grad_probs, axis=0, keepdims=True)
        yield
        stats = jnp.concatenate(
            [*split_pair(total), *split_pair(moment), jnp.zeros((12, TILE), F32)], axis=0
        ).astype(BF16)
        o_ref[j, :, 2 * PAIRS] = stats.reshape(SLICES, 2, TILE)

    for step in range(STEPS):
        for load in loads(step):
            load.wait()
        in_step([head(step * STEP_HEADS + j) for j in range(STEP_HEADS)])


def pack(route, qk, value, grad):
    shape = (HEADS, SLICES, MSG, 2, HEAD_DIM)
    buffer = pltpu.VMEM((TILE, HEADS * HEAD_DIM), BF16)
    hbm = pl.BlockSpec(memory_space=pltpu.HBM)
    return pl.pallas_call(
        pack_kernel,
        out_shape=(
            jax.ShapeDtypeStruct(shape, BF16),
            jax.ShapeDtypeStruct((HEADS, 1), jnp.int32),
            jax.ShapeDtypeStruct((1, TILES), jnp.int32),
        ),
        in_specs=[hbm, hbm, hbm, hbm],
        out_specs=(pl.BlockSpec(memory_space=pltpu.VMEM),) * 3,
        scratch_shapes=[
            pltpu.VMEM((HEADS, TILES), jnp.int32),
            buffer,
            buffer,
            buffer,
            pltpu.SemaphoreType.DMA((STEPS + 1, 3)),
        ],
        compiler_params=pltpu.CompilerParams(vmem_limit_bytes=VMEM_LIMIT),
        name="pack",
    )(*[pltpu.with_memory_space_constraint(x, pltpu.HBM) for x in (route, qk, value, grad)])


def swap_kernel(partner_ref, x_ref, o_ref):
    def move(t, carry):
        o_ref[t] = x_ref[partner_ref[0, t]]
        return carry

    lax.fori_loop(0, TILES, move, 0, unroll=16)


def swap(partner, x):
    whole = pl.BlockSpec(memory_space=pltpu.VMEM)
    return pl.pallas_call(
        swap_kernel,
        out_shape=jax.ShapeDtypeStruct(x.shape, x.dtype),
        in_specs=[pl.BlockSpec(memory_space=pltpu.SMEM), whole],
        out_specs=whole,
        compiler_params=pltpu.CompilerParams(vmem_limit_bytes=VMEM_LIMIT),
        name="swap",
    )(partner, x)


def finish_kernel(upper_ref, qk_ref, v_ref, g_ref, z_ref, out_ref, dqk_ref, dv_ref):
    uppers = upper_ref[...]
    ahead = grid_of(0) - grid_of(1)

    def head(j):
        upper = uppers[j : j + 1, :] != 0
        value = v_ref[:, head_columns(j)]
        grad = g_ref[:, head_columns(j)]
        raw = qk_ref[:, head_columns(j)].astype(F32)
        factor, normed = normalise(raw)
        second = pick(upper, grad, value)
        first = pick(upper, value, grad)
        their_normed = z_ref[j, :, 0:PAIRS].reshape(TILE, HEAD_DIM)
        their_second = z_ref[j, :, PAIRS : 2 * PAIRS].reshape(TILE, HEAD_DIM)
        stats = z_ref[j, :, 2 * PAIRS].reshape(2 * SLICES, TILE).astype(F32)
        their_total = stats[0:1] + stats[1:2]
        their_moment = stats[2:3] + stats[3:4]
        keys = jnp.concatenate([normed, their_normed], axis=0)
        others = jnp.concatenate([first, their_second], axis=0)
        yield
        weights = jnp.exp2(dot_nt(normed, keys) * SCALE_LOG2)
        grad_probs = dot_nt(second, others)
        yield
        inside = jnp.where(upper, ahead, -ahead) >= 0
        own_w = jnp.where(inside, weights[:, :TILE], 0.0)
        cross_w = weights[:, TILE:]
        own_g = grad_probs[:, :TILE]
        cross_g = grad_probs[:, TILE:]
        inv_row = 1.0 / jnp.sum(own_w + cross_w, axis=1, keepdims=True)
        own_inv = 1.0 / jnp.sum(own_w, axis=0, keepdims=True)
        cross_inv = 1.0 / (their_total + jnp.sum(cross_w, axis=0, keepdims=True))
        yield
        own_p = (own_w * jnp.where(upper, inv_row, own_inv)).astype(BF16)
        cross_p = (cross_w * jnp.where(upper, inv_row, cross_inv)).astype(BF16)
        own_f = own_p.astype(F32)
        cross_f = cross_p.astype(F32)
        own_t = own_f * own_g
        cross_t = cross_f * cross_g
        yield
        row_sum = jnp.sum(own_t + cross_t, axis=1, keepdims=True)
        own_sum = jnp.sum(own_t, axis=0, keepdims=True)
        cross_sum = their_moment * cross_inv + jnp.sum(cross_t, axis=0, keepdims=True)
        yield
        own_s = own_f * (own_g - jnp.where(upper, row_sum, own_sum))
        cross_s = cross_f * (cross_g - jnp.where(upper, row_sum, cross_sum))
        own_s = own_s.astype(BF16)
        scores = jnp.concatenate([own_s, cross_s.astype(BF16)], axis=1)
        along = dot_nn(jnp.concatenate([own_p, cross_p], axis=1), others)
        across = dot_tn(own_p, second)
        grad_normed = dot_nn(scores, keys) + dot_tn(own_s, normed)
        yield
        out_ref[:, head_columns(j)] = jnp.where(upper, along, across).astype(BF16)
        dv_ref[:, head_columns(j)] = jnp.where(upper, across, along).astype(BF16)
        grad_normed = (grad_normed * SCALE).astype(BF16).astype(F32)
        inner = jnp.mean(raw * grad_normed, axis=-1, keepdims=True)
        grad_input = factor * grad_normed - raw * (factor**3 * inner)
        dqk_ref[:, head_columns(j)] = grad_input.astype(BF16)

    for start in range(0, HEADS, GROUP):
        in_step([head(start + j) for j in range(GROUP)])


def finish(upper, qk, value, grad, z):
    shape = jax.ShapeDtypeStruct((TILE, HEADS * HEAD_DIM), BF16)
    whole = pl.BlockSpec(memory_space=pltpu.VMEM)
    return pl.pallas_call(
        finish_kernel,
        out_shape=(shape, shape, shape),
        in_specs=[whole] * 5,
        out_specs=(whole, whole, whole),
        compiler_params=pltpu.CompilerParams(vmem_limit_bytes=VMEM_LIMIT),
        name="finish",
    )(upper, qk, value, grad, z)


def deliver_kernel(x_ref, o_hbm, sem):
    copy = pltpu.make_async_copy(x_ref, o_hbm, sem)
    copy.start()
    copy.wait()


def deliver(x):
    return pl.pallas_call(
        deliver_kernel,
        out_shape=pltpu.HBM(x.shape, x.dtype),
        in_specs=[pl.BlockSpec(memory_space=pltpu.VMEM)],
        out_specs=pl.BlockSpec(memory_space=pltpu.HBM),
        scratch_shapes=[pltpu.SemaphoreType.DMA],
        compiler_params=pltpu.CompilerParams(vmem_limit_bytes=VMEM_LIMIT),
        cost_estimate=pl.CostEstimate(
            flops=0, bytes_accessed=2 * x.size * x.dtype.itemsize, transcendentals=0
        ),
        name="deliver",
    )(x)


def exchange(x):
    return lax.all_to_all(x, "seq", split_axis=0, concat_axis=0, tiled=True)


def local(query_key, payload_matrix, out_grad, route_assignment):
    route = route_assignment[0]
    rows = (query_key[0], payload_matrix[0], out_grad[0])
    packed, upper, partner = pack(route.T, *rows)
    slices = exchange(packed.reshape(TILES, MSG, 2, HEAD_DIM))
    theirs = exchange(swap(partner, slices)).reshape(HEADS, SLICES, MSG, 2, HEAD_DIM)
    out, grad_qk, grad_v = finish(upper, *rows, theirs)
    grad_qk, grad_v = lax.ppermute((grad_qk, grad_v), "pipe", [(0, 1), (1, 0)])
    out, grad_qk, grad_v = deliver(out), deliver(grad_qk), deliver(grad_v)
    return (out[None], grad_qk[None], grad_v[None])


def solution(mesh):
    rows = P("pipe", "seq", None)
    return jax.shard_map(
        local,
        mesh=mesh,
        in_specs=(rows, rows, rows, P("pipe", None, None)),
        out_specs=(rows, rows, rows),
        check_vma=False,
    )
```

```python
import math

import jax
import jax.numpy as jnp
from jax import lax
from jax.experimental import pallas as pl
from jax.experimental.pallas import tpu as pltpu
from jax.sharding import PartitionSpec as P

HEADS = 16
HEAD_DIM = 128
TILE = 128
TILES = 128
SLICES = 8
PAIRS = TILE // SLICES // 2
MSG = 2 * PAIRS + 1
STEP_HEADS = 8
STEPS = HEADS // STEP_HEADS
STEP_COLS = STEP_HEADS * HEAD_DIM
EPSILON = 1e-06
SCALE = 4.0 / HEAD_DIM
SCALE_LOG2 = SCALE * math.log2(math.e)
F32 = jnp.float32
BF16 = jnp.bfloat16
GROUP = 8
VMEM_LIMIT = 16 * 1024 * 1024


def dot_nt(a, b):
    return lax.dot_general(a, b, (((1,), (1,)), ((), ())), preferred_element_type=F32)


def dot_nn(a, b):
    return lax.dot_general(a, b, (((1,), (0,)), ((), ())), preferred_element_type=F32)


def dot_tn(a, b):
    return lax.dot_general(a, b, (((0,), (0,)), ((), ())), preferred_element_type=F32)


def split_pair(x):
    high = x.astype(BF16).astype(F32)
    return high, x - high


def normalise(raw):
    factor = lax.rsqrt(jnp.mean(raw * raw, axis=-1, keepdims=True) + EPSILON)
    return factor, (raw * factor).astype(BF16)


def head_columns(j):
    return slice(j * HEAD_DIM, (j + 1) * HEAD_DIM)


def grid_of(axis):
    return lax.broadcasted_iota(jnp.int32, (TILE, TILE), axis)


def pick(upper, if_upper, if_lower):
    return jnp.where(upper, if_upper, if_lower)


def in_step(heads):
    while heads:
        heads = [head for head in heads if next(head, head) is not head]


def pack_kernel(
    route_hbm, qk_hbm, v_hbm, g_hbm, o_ref, upper_ref, partner_ref, route_buf, *scratch
):
    buffers, sems = scratch[:3], scratch[3]
    inputs = (qk_hbm, v_hbm, g_hbm)

    def loads(step):
        span = pl.ds(step * STEP_COLS, STEP_COLS)
        return [
            pltpu.make_async_copy(hbm.at[:, span], buf.at[:, span], sems.at[step, k])
            for k, (hbm, buf) in enumerate(zip(inputs, buffers))
        ]

    route_load = pltpu.make_async_copy(route_hbm, route_buf, sems.at[STEPS, 0])
    route_load.start()
    for step in range(STEPS):
        for load in loads(step):
            load.start()
    qk_buf, v_buf, g_buf = buffers

    route_load.wait()
    me = lax.axis_index("seq")
    route = route_buf[...]
    tiles = lax.broadcasted_iota(jnp.int32, route.shape, 1)
    own = jnp.sum(jnp.where(tiles == me, route, 0), axis=1, keepdims=True)
    earlier = jnp.where((route == own) & (tiles < me), 1.0, 0.0)
    uppers = jnp.max(earlier, axis=1, keepdims=True)
    upper_ref[...] = uppers.astype(jnp.int32)
    heads = lax.broadcasted_iota(jnp.int32, route.shape, 0)
    labels = jnp.sum(jnp.where(heads == me // SLICES, route, 0), axis=0, keepdims=True)
    labels = jnp.broadcast_to(labels, (TILES, TILES))
    diagonal = grid_of(0) == grid_of(1)
    column = jnp.sum(jnp.where(diagonal, labels, 0), axis=1, keepdims=True)
    same = (labels == column) & jnp.logical_not(diagonal)
    partner_ref[...] = jnp.sum(jnp.where(same, grid_of(0), 0), axis=0, keepdims=True)
    at_most = grid_of(0) <= grid_of(1)

    def head(j):
        upper = uppers[j : j + 1, :] > 0.0
        value = v_buf[:, head_columns(j)]
        grad = g_buf[:, head_columns(j)]
        _, normed = normalise(qk_buf[:, head_columns(j)].astype(F32))
        second = pick(upper, grad, value)
        o_ref[j, :, 0:PAIRS] = normed.reshape(SLICES, PAIRS, 2, HEAD_DIM)
        o_ref[j, :, PAIRS : 2 * PAIRS] = second.reshape(SLICES, PAIRS, 2, HEAD_DIM)
        yield
        weights = jnp.where(at_most, jnp.exp2(dot_nt(normed, normed) * SCALE_LOG2), 0.0)
        grad_probs = dot_nt(value, grad)
        yield
        total = jnp.sum(weights, axis=0, keepdims=True)
        moment = jnp.sum(weights * grad_probs, axis=0, keepdims=True)
        yield
        stats = jnp.concatenate(
            [*split_pair(total), *split_pair(moment), jnp.zeros((12, TILE), F32)], axis=0
        ).astype(BF16)
        o_ref[j, :, 2 * PAIRS] = stats.reshape(SLICES, 2, TILE)

    for step in range(STEPS):
        for load in loads(step):
            load.wait()
        in_step([head(step * STEP_HEADS + j) for j in range(STEP_HEADS)])


def pack(route, qk, value, grad):
    shape = (HEADS, SLICES, MSG, 2, HEAD_DIM)
    buffer = pltpu.VMEM((TILE, HEADS * HEAD_DIM), BF16)
    hbm = pl.BlockSpec(memory_space=pltpu.HBM)
    return pl.pallas_call(
        pack_kernel,
        out_shape=(
            jax.ShapeDtypeStruct(shape, BF16),
            jax.ShapeDtypeStruct((HEADS, 1), jnp.int32),
            jax.ShapeDtypeStruct((1, TILES), jnp.int32),
        ),
        in_specs=[hbm, hbm, hbm, hbm],
        out_specs=(pl.BlockSpec(memory_space=pltpu.VMEM),) * 3,
        scratch_shapes=[
            pltpu.VMEM((HEADS, TILES), jnp.int32),
            buffer,
            buffer,
            buffer,
            pltpu.SemaphoreType.DMA((STEPS + 1, 3)),
        ],
        compiler_params=pltpu.CompilerParams(vmem_limit_bytes=VMEM_LIMIT),
        name="pack",
    )(*[pltpu.with_memory_space_constraint(x, pltpu.HBM) for x in (route, qk, value, grad)])


def swap_kernel(partner_ref, x_ref, o_ref):
    def move(t, carry):
        o_ref[t] = x_ref[partner_ref[0, t]]
        return carry

    lax.fori_loop(0, TILES, move, 0, unroll=16)


def swap(partner, x):
    whole = pl.BlockSpec(memory_space=pltpu.VMEM)
    return pl.pallas_call(
        swap_kernel,
        out_shape=jax.ShapeDtypeStruct(x.shape, x.dtype),
        in_specs=[pl.BlockSpec(memory_space=pltpu.SMEM), whole],
        out_specs=whole,
        compiler_params=pltpu.CompilerParams(vmem_limit_bytes=VMEM_LIMIT),
        name="swap",
    )(partner, x)


def finish_kernel(upper_ref, qk_ref, v_ref, g_ref, z_ref, out_ref, dqk_ref, dv_ref):
    uppers = upper_ref[...]
    ahead = grid_of(0) - grid_of(1)

    def head(j):
        upper = uppers[j : j + 1, :] != 0
        value = v_ref[:, head_columns(j)]
        grad = g_ref[:, head_columns(j)]
        raw = qk_ref[:, head_columns(j)].astype(F32)
        factor, normed = normalise(raw)
        second = pick(upper, grad, value)
        first = pick(upper, value, grad)
        their_normed = z_ref[j, :, 0:PAIRS].reshape(TILE, HEAD_DIM)
        their_second = z_ref[j, :, PAIRS : 2 * PAIRS].reshape(TILE, HEAD_DIM)
        stats = z_ref[j, :, 2 * PAIRS].reshape(2 * SLICES, TILE).astype(F32)
        their_total = stats[0:1] + stats[1:2]
        their_moment = stats[2:3] + stats[3:4]
        keys = jnp.concatenate([normed, their_normed], axis=0)
        others = jnp.concatenate([first, their_second], axis=0)
        yield
        scores = [dot_nt(normed, normed), dot_nt(normed, their_normed)]
        weights = jnp.exp2(jnp.concatenate(scores, axis=1) * SCALE_LOG2)
        grad_probs = dot_nt(second, others)
        yield
        inside = jnp.where(upper, ahead, -ahead) >= 0
        own_w = jnp.where(inside, weights[:, :TILE], 0.0)
        cross_w = weights[:, TILE:]
        own_g = grad_probs[:, :TILE]
        cross_g = grad_probs[:, TILE:]
        inv_row = 1.0 / jnp.sum(own_w + cross_w, axis=1, keepdims=True)
        own_inv = 1.0 / jnp.sum(own_w, axis=0, keepdims=True)
        cross_inv = 1.0 / (their_total + jnp.sum(cross_w, axis=0, keepdims=True))
        yield
        own_p = (own_w * jnp.where(upper, inv_row, own_inv)).astype(BF16)
        cross_p = (cross_w * jnp.where(upper, inv_row, cross_inv)).astype(BF16)
        own_f = own_p.astype(F32)
        cross_f = cross_p.astype(F32)
        own_t = own_f * own_g
        cross_t = cross_f * cross_g
        yield
        row_sum = jnp.sum(own_t + cross_t, axis=1, keepdims=True)
        own_sum = jnp.sum(own_t, axis=0, keepdims=True)
        cross_sum = their_moment * cross_inv + jnp.sum(cross_t, axis=0, keepdims=True)
        yield
        own_s = own_f * (own_g - jnp.where(upper, row_sum, own_sum))
        cross_s = cross_f * (cross_g - jnp.where(upper, row_sum, cross_sum))
        own_s = own_s.astype(BF16)
        scores = jnp.concatenate([own_s, cross_s.astype(BF16)], axis=1)
        along = dot_nn(jnp.concatenate([own_p, cross_p], axis=1), others)
        across = dot_tn(own_p, second)
        grad_normed = dot_nn(scores, keys) + dot_tn(own_s, normed)
        yield
        out_ref[:, head_columns(j)] = jnp.where(upper, along, across).astype(BF16)
        dv_ref[:, head_columns(j)] = jnp.where(upper, across, along).astype(BF16)
        grad_normed = (grad_normed * SCALE).astype(BF16).astype(F32)
        inner = jnp.mean(raw * grad_normed, axis=-1, keepdims=True)
        grad_input = factor * grad_normed - raw * (factor**3 * inner)
        dqk_ref[:, head_columns(j)] = grad_input.astype(BF16)

    for start in range(0, HEADS, GROUP):
        in_step([head(start + j) for j in range(GROUP)])


def finish(upper, qk, value, grad, z):
    shape = jax.ShapeDtypeStruct((TILE, HEADS * HEAD_DIM), BF16)
    whole = pl.BlockSpec(memory_space=pltpu.VMEM)
    return pl.pallas_call(
        finish_kernel,
        out_shape=(shape, shape, shape),
        in_specs=[whole] * 5,
        out_specs=(whole, whole, whole),
        compiler_params=pltpu.CompilerParams(vmem_limit_bytes=VMEM_LIMIT),
        name="finish",
    )(upper, qk, value, grad, z)


def deliver_kernel(x_ref, o_hbm, sem):
    copy = pltpu.make_async_copy(x_ref, o_hbm, sem)
    copy.start()
    copy.wait()


def deliver(x):
    return pl.pallas_call(
        deliver_kernel,
        out_shape=pltpu.HBM(x.shape, x.dtype),
        in_specs=[pl.BlockSpec(memory_space=pltpu.VMEM)],
        out_specs=pl.BlockSpec(memory_space=pltpu.HBM),
        scratch_shapes=[pltpu.SemaphoreType.DMA],
        compiler_params=pltpu.CompilerParams(vmem_limit_bytes=VMEM_LIMIT),
        cost_estimate=pl.CostEstimate(
            flops=0, bytes_accessed=2 * x.size * x.dtype.itemsize, transcendentals=0
        ),
        name="deliver",
    )(x)


def exchange(x):
    return lax.all_to_all(x, "seq", split_axis=0, concat_axis=0, tiled=True)


def local(query_key, payload_matrix, out_grad, route_assignment):
    route = route_assignment[0]
    rows = (query_key[0], payload_matrix[0], out_grad[0])
    packed, upper, partner = pack(route.T, *rows)
    slices = exchange(packed.reshape(TILES, MSG, 2, HEAD_DIM))
    theirs = exchange(swap(partner, slices)).reshape(HEADS, SLICES, MSG, 2, HEAD_DIM)
    out, grad_qk, grad_v = finish(upper, *rows, theirs)
    grad_qk, grad_v = lax.ppermute((grad_qk, grad_v), "pipe", [(0, 1), (1, 0)])
    out, grad_qk, grad_v = deliver(out), deliver(grad_qk), deliver(grad_v)
    return (out[None], grad_qk[None], grad_v[None])


def solution(mesh):
    rows = P("pipe", "seq", None)
    return jax.shard_map(
        local,
        mesh=mesh,
        in_specs=(rows, rows, rows, P("pipe", None, None)),
        out_specs=(rows, rows, rows),
        check_vma=False,
    )
```

```python
import math

import jax
import jax.numpy as jnp
from jax import lax
from jax.experimental import pallas as pl
from jax.experimental.pallas import tpu as pltpu
from jax.sharding import PartitionSpec as P

HEADS = 16
HEAD_DIM = 128
TILE = 128
TILES = 128
SLICES = 8
PAIRS = TILE // SLICES // 2
MSG = 2 * PAIRS + 1
STEP_HEADS = 8
STEPS = HEADS // STEP_HEADS
STEP_COLS = STEP_HEADS * HEAD_DIM
EPSILON = 1e-06
SCALE = 4.0 / HEAD_DIM
SCALE_LOG2 = SCALE * math.log2(math.e)
F32 = jnp.float32
BF16 = jnp.bfloat16
GROUP = 8
VMEM_LIMIT = 16 * 1024 * 1024


def dot_nt(a, b):
    return lax.dot_general(a, b, (((1,), (1,)), ((), ())), preferred_element_type=F32)


def dot_nn(a, b):
    return lax.dot_general(a, b, (((1,), (0,)), ((), ())), preferred_element_type=F32)


def dot_tn(a, b):
    return lax.dot_general(a, b, (((0,), (0,)), ((), ())), preferred_element_type=F32)


def split_pair(x):
    high = x.astype(BF16).astype(F32)
    return high, x - high


def normalise(raw):
    factor = lax.rsqrt(jnp.mean(raw * raw, axis=-1, keepdims=True) + EPSILON)
    return factor, (raw * factor).astype(BF16)


def head_columns(j):
    return slice(j * HEAD_DIM, (j + 1) * HEAD_DIM)


def grid_of(axis):
    return lax.broadcasted_iota(jnp.int32, (TILE, TILE), axis)


def pick(upper, if_upper, if_lower):
    return jnp.where(upper, if_upper, if_lower)


def in_step(heads):
    while heads:
        heads = [head for head in heads if next(head, head) is not head]


def pack_kernel(
    route_hbm, qk_hbm, v_hbm, g_hbm, o_ref, upper_ref, partner_smem, route_buf, partner_buf, *scratch
):
    buffers, sems = scratch[:3], scratch[3]
    inputs = (qk_hbm, v_hbm, g_hbm)

    def loads(step):
        span = pl.ds(step * STEP_COLS, STEP_COLS)
        return [
            pltpu.make_async_copy(hbm.at[:, span], buf.at[:, span], sems.at[step, k])
            for k, (hbm, buf) in enumerate(zip(inputs, buffers))
        ]

    route_load = pltpu.make_async_copy(route_hbm, route_buf, sems.at[STEPS, 0])
    route_load.start()
    for step in range(STEPS):
        for load in loads(step):
            load.start()
    qk_buf, v_buf, g_buf = buffers

    route_load.wait()
    me = lax.axis_index("seq")
    route = route_buf[...]
    tiles = lax.broadcasted_iota(jnp.int32, route.shape, 1)
    own = jnp.sum(jnp.where(tiles == me, route, 0), axis=1, keepdims=True)
    earlier = jnp.where((route == own) & (tiles < me), 1.0, 0.0)
    uppers = jnp.max(earlier, axis=1, keepdims=True)
    upper_ref[...] = uppers.astype(jnp.int32)
    heads = lax.broadcasted_iota(jnp.int32, route.shape, 0)
    labels = jnp.sum(jnp.where(heads == me // SLICES, route, 0), axis=0, keepdims=True)
    labels = jnp.broadcast_to(labels, (TILES, TILES))
    diagonal = grid_of(0) == grid_of(1)
    column = jnp.sum(jnp.where(diagonal, labels, 0), axis=1, keepdims=True)
    same = (labels == column) & jnp.logical_not(diagonal)
    partner_buf[...] = jnp.sum(jnp.where(same, grid_of(0), 0), axis=0, keepdims=True)
    partner_store = pltpu.make_async_copy(partner_buf, partner_smem, sems.at[STEPS, 1])
    partner_store.start()
    at_most = grid_of(0) <= grid_of(1)

    def head(j):
        upper = uppers[j : j + 1, :] > 0.0
        value = v_buf[:, head_columns(j)]
        grad = g_buf[:, head_columns(j)]
        _, normed = normalise(qk_buf[:, head_columns(j)].astype(F32))
        second = pick(upper, grad, value)
        o_ref[j, :, 0:PAIRS] = normed.reshape(SLICES, PAIRS, 2, HEAD_DIM)
        o_ref[j, :, PAIRS : 2 * PAIRS] = second.reshape(SLICES, PAIRS, 2, HEAD_DIM)
        yield
        weights = jnp.where(at_most, jnp.exp2(dot_nt(normed, normed) * SCALE_LOG2), 0.0)
        grad_probs = dot_nt(value, grad)
        yield
        total = jnp.sum(weights, axis=0, keepdims=True)
        moment = jnp.sum(weights * grad_probs, axis=0, keepdims=True)
        yield
        stats = jnp.concatenate(
            [*split_pair(total), *split_pair(moment), jnp.zeros((12, TILE), F32)], axis=0
        ).astype(BF16)
        o_ref[j, :, 2 * PAIRS] = stats.reshape(SLICES, 2, TILE)

    for step in range(STEPS):
        for load in loads(step):
            load.wait()
        in_step([head(step * STEP_HEADS + j) for j in range(STEP_HEADS)])
    partner_store.wait()


def pack(route, qk, value, grad):
    shape = (HEADS, SLICES, MSG, 2, HEAD_DIM)
    buffer = pltpu.VMEM((TILE, HEADS * HEAD_DIM), BF16)
    hbm = pl.BlockSpec(memory_space=pltpu.HBM)
    whole = pl.BlockSpec(memory_space=pltpu.VMEM)
    return pl.pallas_call(
        pack_kernel,
        out_shape=(
            jax.ShapeDtypeStruct(shape, BF16),
            jax.ShapeDtypeStruct((HEADS, 1), jnp.int32),
            pltpu.SMEM((1, TILES), jnp.int32),
        ),
        in_specs=[hbm, hbm, hbm, hbm],
        out_specs=(whole, whole, pl.BlockSpec(memory_space=pltpu.SMEM)),
        scratch_shapes=[
            pltpu.VMEM((HEADS, TILES), jnp.int32),
            pltpu.VMEM((1, TILES), jnp.int32),
            buffer,
            buffer,
            buffer,
            pltpu.SemaphoreType.DMA((STEPS + 1, 3)),
        ],
        compiler_params=pltpu.CompilerParams(vmem_limit_bytes=VMEM_LIMIT),
        name="pack",
    )(*[pltpu.with_memory_space_constraint(x, pltpu.HBM) for x in (route, qk, value, grad)])


def swap_kernel(partner_ref, x_ref, o_ref):
    def move(t, carry):
        o_ref[t] = x_ref[partner_ref[0, t]]
        return carry

    lax.fori_loop(0, TILES, move, 0, unroll=16)


def swap(partner, x):
    whole = pl.BlockSpec(memory_space=pltpu.VMEM)
    return pl.pallas_call(
        swap_kernel,
        out_shape=jax.ShapeDtypeStruct(x.shape, x.dtype),
        in_specs=[pl.BlockSpec(memory_space=pltpu.SMEM), whole],
        out_specs=whole,
        compiler_params=pltpu.CompilerParams(vmem_limit_bytes=VMEM_LIMIT),
        name="swap",
    )(pltpu.with_memory_space_constraint(partner, pltpu.SMEM), x)


def finish_kernel(upper_ref, qk_ref, v_ref, g_ref, z_ref, out_ref, dqk_ref, dv_ref):
    uppers = upper_ref[...]
    ahead = grid_of(0) - grid_of(1)

    def head(j):
        upper = uppers[j : j + 1, :] != 0
        value = v_ref[:, head_columns(j)]
        grad = g_ref[:, head_columns(j)]
        raw = qk_ref[:, head_columns(j)].astype(F32)
        factor, normed = normalise(raw)
        second = pick(upper, grad, value)
        first = pick(upper, value, grad)
        their_normed = z_ref[j, :, 0:PAIRS].reshape(TILE, HEAD_DIM)
        their_second = z_ref[j, :, PAIRS : 2 * PAIRS].reshape(TILE, HEAD_DIM)
        stats = z_ref[j, :, 2 * PAIRS].reshape(2 * SLICES, TILE).astype(F32)
        their_total = stats[0:1] + stats[1:2]
        their_moment = stats[2:3] + stats[3:4]
        keys = jnp.concatenate([normed, their_normed], axis=0)
        others = jnp.concatenate([first, their_second], axis=0)
        yield
        scores = [dot_nt(normed, normed), dot_nt(normed, their_normed)]
        weights = jnp.exp2(jnp.concatenate(scores, axis=1) * SCALE_LOG2)
        grad_probs = dot_nt(second, others)
        yield
        inside = jnp.where(upper, ahead, -ahead) >= 0
        own_w = jnp.where(inside, weights[:, :TILE], 0.0)
        cross_w = weights[:, TILE:]
        own_g = grad_probs[:, :TILE]
        cross_g = grad_probs[:, TILE:]
        inv_row = 1.0 / jnp.sum(own_w + cross_w, axis=1, keepdims=True)
        own_inv = 1.0 / jnp.sum(own_w, axis=0, keepdims=True)
        cross_inv = 1.0 / (their_total + jnp.sum(cross_w, axis=0, keepdims=True))
        yield
        own_p = (own_w * jnp.where(upper, inv_row, own_inv)).astype(BF16)
        cross_p = (cross_w * jnp.where(upper, inv_row, cross_inv)).astype(BF16)
        own_f = own_p.astype(F32)
        cross_f = cross_p.astype(F32)
        own_t = own_f * own_g
        cross_t = cross_f * cross_g
        yield
        row_sum = jnp.sum(own_t + cross_t, axis=1, keepdims=True)
        own_sum = jnp.sum(own_t, axis=0, keepdims=True)
        cross_sum = their_moment * cross_inv + jnp.sum(cross_t, axis=0, keepdims=True)
        yield
        own_s = own_f * (own_g - jnp.where(upper, row_sum, own_sum))
        cross_s = cross_f * (cross_g - jnp.where(upper, row_sum, cross_sum))
        own_s = own_s.astype(BF16)
        scores = jnp.concatenate([own_s, cross_s.astype(BF16)], axis=1)
        along = dot_nn(jnp.concatenate([own_p, cross_p], axis=1), others)
        across = dot_tn(own_p, second)
        grad_normed = dot_nn(scores, keys) + dot_tn(own_s, normed)
        yield
        out_ref[:, head_columns(j)] = jnp.where(upper, along, across).astype(BF16)
        dv_ref[:, head_columns(j)] = jnp.where(upper, across, along).astype(BF16)
        grad_normed = (grad_normed * SCALE).astype(BF16).astype(F32)
        inner = jnp.mean(raw * grad_normed, axis=-1, keepdims=True)
        grad_input = factor * grad_normed - raw * (factor**3 * inner)
        dqk_ref[:, head_columns(j)] = grad_input.astype(BF16)

    for start in range(0, HEADS, GROUP):
        in_step([head(start + j) for j in range(GROUP)])


def finish(upper, qk, value, grad, z):
    shape = jax.ShapeDtypeStruct((TILE, HEADS * HEAD_DIM), BF16)
    whole = pl.BlockSpec(memory_space=pltpu.VMEM)
    return pl.pallas_call(
        finish_kernel,
        out_shape=(shape, shape, shape),
        in_specs=[whole] * 5,
        out_specs=(whole, whole, whole),
        compiler_params=pltpu.CompilerParams(vmem_limit_bytes=VMEM_LIMIT),
        name="finish",
    )(upper, qk, value, grad, z)


def deliver_kernel(x_ref, o_hbm, sem):
    copy = pltpu.make_async_copy(x_ref, o_hbm, sem)
    copy.start()
    copy.wait()


def deliver(x):
    return pl.pallas_call(
        deliver_kernel,
        out_shape=pltpu.HBM(x.shape, x.dtype),
        in_specs=[pl.BlockSpec(memory_space=pltpu.VMEM)],
        out_specs=pl.BlockSpec(memory_space=pltpu.HBM),
        scratch_shapes=[pltpu.SemaphoreType.DMA],
        compiler_params=pltpu.CompilerParams(vmem_limit_bytes=VMEM_LIMIT),
        cost_estimate=pl.CostEstimate(
            flops=0, bytes_accessed=2 * x.size * x.dtype.itemsize, transcendentals=0
        ),
        name="deliver",
    )(x)


def exchange(x):
    return lax.all_to_all(x, "seq", split_axis=0, concat_axis=0, tiled=True)


def local(query_key, payload_matrix, out_grad, route_assignment):
    route = route_assignment[0]
    rows = (query_key[0], payload_matrix[0], out_grad[0])
    packed, upper, partner = pack(route.T, *rows)
    slices = exchange(packed.reshape(TILES, MSG, 2, HEAD_DIM))
    theirs = exchange(swap(partner, slices)).reshape(HEADS, SLICES, MSG, 2, HEAD_DIM)
    out, grad_qk, grad_v = finish(upper, *rows, theirs)
    grad_qk, grad_v = lax.ppermute((grad_qk, grad_v), "pipe", [(0, 1), (1, 0)])
    out, grad_qk, grad_v = deliver(out), deliver(grad_qk), deliver(grad_v)
    return (out[None], grad_qk[None], grad_v[None])


def solution(mesh):
    rows = P("pipe", "seq", None)
    return jax.shard_map(
        local,
        mesh=mesh,
        in_specs=(rows, rows, rows, P("pipe", None, None)),
        out_specs=(rows, rows, rows),
        check_vma=False,
    )
```

```python
import math

import jax
import jax.numpy as jnp
from jax import lax
from jax.experimental import pallas as pl
from jax.experimental.pallas import tpu as pltpu
from jax.sharding import PartitionSpec as P

HEADS = 16
HEAD_DIM = 128
TILE = 128
TILES = 128
SLICES = 8
PAIRS = TILE // SLICES // 2
MSG = 2 * PAIRS + 1
STEP_HEADS = 16
STEPS = HEADS // STEP_HEADS
STEP_COLS = STEP_HEADS * HEAD_DIM
EPSILON = 1e-06
SCALE = 4.0 / HEAD_DIM
SCALE_LOG2 = SCALE * math.log2(math.e)
F32 = jnp.float32
BF16 = jnp.bfloat16
GROUP = 8
VMEM_LIMIT = 16 * 1024 * 1024


def dot_nt(a, b):
    return lax.dot_general(a, b, (((1,), (1,)), ((), ())), preferred_element_type=F32)


def dot_nn(a, b):
    return lax.dot_general(a, b, (((1,), (0,)), ((), ())), preferred_element_type=F32)


def dot_tn(a, b):
    return lax.dot_general(a, b, (((0,), (0,)), ((), ())), preferred_element_type=F32)


def split_pair(x):
    high = x.astype(BF16).astype(F32)
    return high, x - high


def normalise(raw):
    factor = lax.rsqrt(jnp.mean(raw * raw, axis=-1, keepdims=True) + EPSILON)
    return factor, (raw * factor).astype(BF16)


def head_columns(j):
    return slice(j * HEAD_DIM, (j + 1) * HEAD_DIM)


def grid_of(axis):
    return lax.broadcasted_iota(jnp.int32, (TILE, TILE), axis)


def pick(upper, if_upper, if_lower):
    return jnp.where(upper, if_upper, if_lower)


def in_step(heads):
    while heads:
        heads = [head for head in heads if next(head, head) is not head]


def pack_kernel(
    route_hbm, qk_hbm, v_hbm, g_hbm, o_ref, upper_ref, partner_smem, route_buf, partner_buf, *scratch
):
    buffers, sems = scratch[:3], scratch[3]
    inputs = (qk_hbm, v_hbm, g_hbm)

    def loads(step):
        span = pl.ds(step * STEP_COLS, STEP_COLS)
        return [
            pltpu.make_async_copy(hbm.at[:, span], buf.at[:, span], sems.at[step, k])
            for k, (hbm, buf) in enumerate(zip(inputs, buffers))
        ]

    route_load = pltpu.make_async_copy(route_hbm, route_buf, sems.at[STEPS, 0])
    route_load.start()
    for step in range(STEPS):
        for load in loads(step):
            load.start()
    qk_buf, v_buf, g_buf = buffers

    route_load.wait()
    me = lax.axis_index("seq")
    route = route_buf[...]
    tiles = lax.broadcasted_iota(jnp.int32, route.shape, 1)
    own = jnp.sum(jnp.where(tiles == me, route, 0), axis=1, keepdims=True)
    earlier = jnp.where((route == own) & (tiles < me), 1.0, 0.0)
    uppers = jnp.max(earlier, axis=1, keepdims=True)
    upper_ref[...] = uppers.astype(jnp.int32)
    heads = lax.broadcasted_iota(jnp.int32, route.shape, 0)
    labels = jnp.sum(jnp.where(heads == me // SLICES, route, 0), axis=0, keepdims=True)
    labels = jnp.broadcast_to(labels, (TILES, TILES))
    diagonal = grid_of(0) == grid_of(1)
    column = jnp.sum(jnp.where(diagonal, labels, 0), axis=1, keepdims=True)
    same = (labels == column) & jnp.logical_not(diagonal)
    partner_buf[...] = jnp.sum(jnp.where(same, grid_of(0), 0), axis=0, keepdims=True)
    partner_store = pltpu.make_async_copy(partner_buf, partner_smem, sems.at[STEPS, 1])
    partner_store.start()
    at_most = grid_of(0) <= grid_of(1)

    def head(j):
        upper = uppers[j : j + 1, :] > 0.0
        _, normed = normalise(qk_buf[:, head_columns(j)].astype(F32))
        o_ref[j, :, 0:PAIRS] = normed.reshape(SLICES, PAIRS, 2, HEAD_DIM)
        yield
        value = v_buf[:, head_columns(j)]
        grad = g_buf[:, head_columns(j)]
        second = pick(upper, grad, value)
        o_ref[j, :, PAIRS : 2 * PAIRS] = second.reshape(SLICES, PAIRS, 2, HEAD_DIM)
        weights = jnp.where(at_most, jnp.exp2(dot_nt(normed, normed) * SCALE_LOG2), 0.0)
        grad_probs = dot_nt(value, grad)
        yield
        total = jnp.sum(weights, axis=0, keepdims=True)
        moment = jnp.sum(weights * grad_probs, axis=0, keepdims=True)
        yield
        stats = jnp.concatenate(
            [*split_pair(total), *split_pair(moment), jnp.zeros((12, TILE), F32)], axis=0
        ).astype(BF16)
        o_ref[j, :, 2 * PAIRS] = stats.reshape(SLICES, 2, TILE)

    for step in range(STEPS):
        qk_load, *other_loads = loads(step)
        qk_load.wait()
        heads_here = [head(step * STEP_HEADS + j) for j in range(STEP_HEADS)]
        for one in heads_here:
            next(one)
        for load in other_loads:
            load.wait()
        in_step(heads_here)
    partner_store.wait()


def pack(route, qk, value, grad):
    shape = (HEADS, SLICES, MSG, 2, HEAD_DIM)
    buffer = pltpu.VMEM((TILE, HEADS * HEAD_DIM), BF16)
    hbm = pl.BlockSpec(memory_space=pltpu.HBM)
    whole = pl.BlockSpec(memory_space=pltpu.VMEM)
    return pl.pallas_call(
        pack_kernel,
        out_shape=(
            jax.ShapeDtypeStruct(shape, BF16),
            jax.ShapeDtypeStruct((HEADS, 1), jnp.int32),
            pltpu.SMEM((1, TILES), jnp.int32),
        ),
        in_specs=[hbm, hbm, hbm, hbm],
        out_specs=(whole, whole, pl.BlockSpec(memory_space=pltpu.SMEM)),
        scratch_shapes=[
            pltpu.VMEM((HEADS, TILES), jnp.int32),
            pltpu.VMEM((1, TILES), jnp.int32),
            buffer,
            buffer,
            buffer,
            pltpu.SemaphoreType.DMA((STEPS + 1, 3)),
        ],
        compiler_params=pltpu.CompilerParams(vmem_limit_bytes=VMEM_LIMIT),
        name="pack",
    )(*[pltpu.with_memory_space_constraint(x, pltpu.HBM) for x in (route, qk, value, grad)])


def swap_kernel(partner_ref, x_ref, o_ref):
    def move(t, carry):
        o_ref[t] = x_ref[partner_ref[0, t]]
        return carry

    lax.fori_loop(0, TILES, move, 0, unroll=16)


def swap(partner, x):
    whole = pl.BlockSpec(memory_space=pltpu.VMEM)
    return pl.pallas_call(
        swap_kernel,
        out_shape=jax.ShapeDtypeStruct(x.shape, x.dtype),
        in_specs=[pl.BlockSpec(memory_space=pltpu.SMEM), whole],
        out_specs=whole,
        compiler_params=pltpu.CompilerParams(vmem_limit_bytes=VMEM_LIMIT),
        name="swap",
    )(pltpu.with_memory_space_constraint(partner, pltpu.SMEM), x)


def finish_kernel(upper_ref, qk_ref, v_ref, g_ref, z_ref, out_ref, dqk_ref, dv_ref):
    uppers = upper_ref[...]
    ahead = grid_of(0) - grid_of(1)

    def head(j):
        upper = uppers[j : j + 1, :] != 0
        value = v_ref[:, head_columns(j)]
        grad = g_ref[:, head_columns(j)]
        raw = qk_ref[:, head_columns(j)].astype(F32)
        factor, normed = normalise(raw)
        second = pick(upper, grad, value)
        first = pick(upper, value, grad)
        their_normed = z_ref[j, :, 0:PAIRS].reshape(TILE, HEAD_DIM)
        their_second = z_ref[j, :, PAIRS : 2 * PAIRS].reshape(TILE, HEAD_DIM)
        stats = z_ref[j, :, 2 * PAIRS].reshape(2 * SLICES, TILE).astype(F32)
        their_total = stats[0:1] + stats[1:2]
        their_moment = stats[2:3] + stats[3:4]
        keys = jnp.concatenate([normed, their_normed], axis=0)
        others = jnp.concatenate([first, their_second], axis=0)
        yield
        scores = [dot_nt(normed, normed), dot_nt(normed, their_normed)]
        weights = jnp.exp2(jnp.concatenate(scores, axis=1) * SCALE_LOG2)
        grad_probs = dot_nt(second, others)
        yield
        inside = jnp.where(upper, ahead, -ahead) >= 0
        own_w = jnp.where(inside, weights[:, :TILE], 0.0)
        cross_w = weights[:, TILE:]
        own_g = grad_probs[:, :TILE]
        cross_g = grad_probs[:, TILE:]
        inv_row = 1.0 / jnp.sum(own_w + cross_w, axis=1, keepdims=True)
        own_inv = 1.0 / jnp.sum(own_w, axis=0, keepdims=True)
        cross_inv = 1.0 / (their_total + jnp.sum(cross_w, axis=0, keepdims=True))
        yield
        own_p = (own_w * jnp.where(upper, inv_row, own_inv)).astype(BF16)
        cross_p = (cross_w * jnp.where(upper, inv_row, cross_inv)).astype(BF16)
        own_f = own_p.astype(F32)
        cross_f = cross_p.astype(F32)
        own_t = own_f * own_g
        cross_t = cross_f * cross_g
        yield
        row_sum = jnp.sum(own_t + cross_t, axis=1, keepdims=True)
        own_sum = jnp.sum(own_t, axis=0, keepdims=True)
        cross_sum = their_moment * cross_inv + jnp.sum(cross_t, axis=0, keepdims=True)
        yield
        own_s = own_f * (own_g - jnp.where(upper, row_sum, own_sum))
        cross_s = cross_f * (cross_g - jnp.where(upper, row_sum, cross_sum))
        own_s = own_s.astype(BF16)
        scores = jnp.concatenate([own_s, cross_s.astype(BF16)], axis=1)
        along = dot_nn(jnp.concatenate([own_p, cross_p], axis=1), others)
        across = dot_tn(own_p, second)
        grad_normed = dot_nn(scores, keys) + dot_tn(own_s, normed)
        yield
        out_ref[:, head_columns(j)] = jnp.where(upper, along, across).astype(BF16)
        dv_ref[:, head_columns(j)] = jnp.where(upper, across, along).astype(BF16)
        grad_normed = (grad_normed * SCALE).astype(BF16).astype(F32)
        inner = jnp.mean(raw * grad_normed, axis=-1, keepdims=True)
        grad_input = factor * grad_normed - raw * (factor**3 * inner)
        dqk_ref[:, head_columns(j)] = grad_input.astype(BF16)

    for start in range(0, HEADS, GROUP):
        in_step([head(start + j) for j in range(GROUP)])


def finish(upper, qk, value, grad, z):
    shape = jax.ShapeDtypeStruct((TILE, HEADS * HEAD_DIM), BF16)
    whole = pl.BlockSpec(memory_space=pltpu.VMEM)
    return pl.pallas_call(
        finish_kernel,
        out_shape=(shape, shape, shape),
        in_specs=[whole] * 5,
        out_specs=(whole, whole, whole),
        compiler_params=pltpu.CompilerParams(vmem_limit_bytes=VMEM_LIMIT),
        name="finish",
    )(upper, qk, value, grad, z)


def deliver_kernel(x_ref, o_hbm, sem):
    copy = pltpu.make_async_copy(x_ref, o_hbm, sem)
    copy.start()
    copy.wait()


def deliver(x):
    return pl.pallas_call(
        deliver_kernel,
        out_shape=pltpu.HBM(x.shape, x.dtype),
        in_specs=[pl.BlockSpec(memory_space=pltpu.VMEM)],
        out_specs=pl.BlockSpec(memory_space=pltpu.HBM),
        scratch_shapes=[pltpu.SemaphoreType.DMA],
        compiler_params=pltpu.CompilerParams(vmem_limit_bytes=VMEM_LIMIT),
        cost_estimate=pl.CostEstimate(
            flops=0, bytes_accessed=2 * x.size * x.dtype.itemsize, transcendentals=0
        ),
        name="deliver",
    )(x)


def exchange(x):
    return lax.all_to_all(x, "seq", split_axis=0, concat_axis=0, tiled=True)


def local(query_key, payload_matrix, out_grad, route_assignment):
    route = route_assignment[0]
    rows = (query_key[0], payload_matrix[0], out_grad[0])
    packed, upper, partner = pack(route.T, *rows)
    slices = exchange(packed.reshape(TILES, MSG, 2, HEAD_DIM))
    theirs = exchange(swap(partner, slices)).reshape(HEADS, SLICES, MSG, 2, HEAD_DIM)
    out, grad_qk, grad_v = finish(upper, *rows, theirs)
    grad_qk, grad_v = lax.ppermute((grad_qk, grad_v), "pipe", [(0, 1), (1, 0)])
    out, grad_qk, grad_v = deliver(out), deliver(grad_qk), deliver(grad_v)
    return (out[None], grad_qk[None], grad_v[None])


def solution(mesh):
    rows = P("pipe", "seq", None)
    return jax.shard_map(
        local,
        mesh=mesh,
        in_specs=(rows, rows, rows, P("pipe", None, None)),
        out_specs=(rows, rows, rows),
        check_vma=False,
    )
```

```python
import math

import jax
import jax.numpy as jnp
from jax import lax
from jax.experimental import pallas as pl
from jax.experimental.pallas import tpu as pltpu
from jax.sharding import PartitionSpec as P

HEADS = 16
HEAD_DIM = 128
TILE = 128
TILES = 128
SLICES = 8
PAIRS = TILE // SLICES // 2
MSG = 2 * PAIRS + 1
STEP_HEADS = 16
STEPS = HEADS // STEP_HEADS
STEP_COLS = STEP_HEADS * HEAD_DIM
EPSILON = 1e-06
SCALE = 4.0 / HEAD_DIM
SCALE_LOG2 = SCALE * math.log2(math.e)
F32 = jnp.float32
BF16 = jnp.bfloat16
GROUP = 8
VMEM_LIMIT = 16 * 1024 * 1024


def dot_nt(a, b):
    return lax.dot_general(a, b, (((1,), (1,)), ((), ())), preferred_element_type=F32)


def dot_nn(a, b):
    return lax.dot_general(a, b, (((1,), (0,)), ((), ())), preferred_element_type=F32)


def dot_tn(a, b):
    return lax.dot_general(a, b, (((0,), (0,)), ((), ())), preferred_element_type=F32)


def split_pair(x):
    high = x.astype(BF16).astype(F32)
    return high, x - high


def normalise(raw):
    factor = lax.rsqrt(jnp.mean(raw * raw, axis=-1, keepdims=True) + EPSILON)
    return factor, (raw * factor).astype(BF16)


def head_columns(j):
    return slice(j * HEAD_DIM, (j + 1) * HEAD_DIM)


def grid_of(axis):
    return lax.broadcasted_iota(jnp.int32, (TILE, TILE), axis)


def pick(upper, if_upper, if_lower):
    return jnp.where(upper, if_upper, if_lower)


def in_step(heads):
    while heads:
        heads = [head for head in heads if next(head, head) is not head]


def pack_kernel(
    route_hbm, qk_hbm, v_hbm, g_hbm, o_ref, upper_ref, partner_smem, route_buf, partner_buf, *scratch
):
    buffers, sems = scratch[:3], scratch[3]
    inputs = (qk_hbm, v_hbm, g_hbm)

    def loads(step):
        span = pl.ds(step * STEP_COLS, STEP_COLS)
        return [
            pltpu.make_async_copy(hbm.at[:, span], buf.at[:, span], sems.at[step, k])
            for k, (hbm, buf) in enumerate(zip(inputs, buffers))
        ]

    route_load = pltpu.make_async_copy(route_hbm, route_buf, sems.at[STEPS, 0])
    route_load.start()
    for step in range(STEPS):
        for load in loads(step):
            load.start()
    qk_buf, v_buf, g_buf = buffers

    route_load.wait()
    me = lax.axis_index("seq")
    route = route_buf[...]
    tiles = lax.broadcasted_iota(jnp.int32, route.shape, 1)
    own = jnp.sum(jnp.where(tiles == me, route, 0), axis=1, keepdims=True)
    earlier = jnp.where((route == own) & (tiles < me), 1.0, 0.0)
    uppers = jnp.max(earlier, axis=1, keepdims=True)
    upper_ref[...] = uppers.astype(jnp.int32)
    heads = lax.broadcasted_iota(jnp.int32, route.shape, 0)
    labels = jnp.sum(jnp.where(heads == me // SLICES, route, 0), axis=0, keepdims=True)
    labels = jnp.broadcast_to(labels, (TILES, TILES))
    diagonal = grid_of(0) == grid_of(1)
    column = jnp.sum(jnp.where(diagonal, labels, 0), axis=1, keepdims=True)
    same = (labels == column) & jnp.logical_not(diagonal)
    partner_buf[...] = jnp.sum(jnp.where(same, grid_of(0), 0), axis=0, keepdims=True)
    partner_store = pltpu.make_async_copy(partner_buf, partner_smem, sems.at[STEPS, 1])
    partner_store.start()
    at_most = grid_of(0) <= grid_of(1)

    def head(j):
        upper = uppers[j : j + 1, :] > 0.0
        _, normed = normalise(qk_buf[:, head_columns(j)].astype(F32))
        o_ref[j, :, 0:PAIRS] = normed.reshape(SLICES, PAIRS, 2, HEAD_DIM)
        yield
        value = v_buf[:, head_columns(j)]
        grad = g_buf[:, head_columns(j)]
        second = pick(upper, grad, value)
        o_ref[j, :, PAIRS : 2 * PAIRS] = second.reshape(SLICES, PAIRS, 2, HEAD_DIM)
        weights = jnp.where(at_most, jnp.exp2(dot_nt(normed, normed) * SCALE_LOG2), 0.0)
        grad_probs = dot_nt(value, grad)
        yield
        total = jnp.sum(weights, axis=0, keepdims=True)
        moment = jnp.sum(weights * grad_probs, axis=0, keepdims=True)
        yield
        stats = jnp.concatenate(
            [*split_pair(total), *split_pair(moment), jnp.zeros((12, TILE), F32)], axis=0
        ).astype(BF16)
        o_ref[j, :, 2 * PAIRS] = stats.reshape(SLICES, 2, TILE)

    for step in range(STEPS):
        qk_load, *other_loads = loads(step)
        qk_load.wait()
        heads_here = [head(step * STEP_HEADS + j) for j in range(STEP_HEADS)]
        for one in heads_here:
            next(one)
        for load in other_loads:
            load.wait()
        in_step(heads_here)
    partner_store.wait()


def pack(route, qk, value, grad):
    shape = (HEADS, SLICES, MSG, 2, HEAD_DIM)
    buffer = pltpu.VMEM((TILE, HEADS * HEAD_DIM), BF16)
    hbm = pl.BlockSpec(memory_space=pltpu.HBM)
    whole = pl.BlockSpec(memory_space=pltpu.VMEM)
    return pl.pallas_call(
        pack_kernel,
        out_shape=(
            jax.ShapeDtypeStruct(shape, BF16),
            jax.ShapeDtypeStruct((HEADS, 1), jnp.int32),
            pltpu.SMEM((1, TILES), jnp.int32),
        ),
        in_specs=[hbm, hbm, hbm, hbm],
        out_specs=(whole, whole, pl.BlockSpec(memory_space=pltpu.SMEM)),
        scratch_shapes=[
            pltpu.VMEM((HEADS, TILES), jnp.int32),
            pltpu.VMEM((1, TILES), jnp.int32),
            buffer,
            buffer,
            buffer,
            pltpu.SemaphoreType.DMA((STEPS + 1, 3)),
        ],
        compiler_params=pltpu.CompilerParams(vmem_limit_bytes=VMEM_LIMIT),
        name="pack",
    )(*[pltpu.with_memory_space_constraint(x, pltpu.HBM) for x in (route, qk, value, grad)])


def swap_kernel(partner_ref, x_ref, o_ref):
    def move(t, carry):
        o_ref[t] = x_ref[partner_ref[0, t]]
        return carry

    lax.fori_loop(0, TILES, move, 0, unroll=16)


def swap(partner, x):
    whole = pl.BlockSpec(memory_space=pltpu.VMEM)
    return pl.pallas_call(
        swap_kernel,
        out_shape=jax.ShapeDtypeStruct(x.shape, x.dtype),
        in_specs=[pl.BlockSpec(memory_space=pltpu.SMEM), whole],
        out_specs=whole,
        compiler_params=pltpu.CompilerParams(vmem_limit_bytes=VMEM_LIMIT),
        name="swap",
    )(pltpu.with_memory_space_constraint(partner, pltpu.SMEM), x)


def finish_kernel(upper_ref, qk_ref, v_ref, g_ref, z_ref, out_ref, grads_ref):
    uppers = upper_ref[...]
    ahead = grid_of(0) - grid_of(1)

    def head(j):
        upper = uppers[j : j + 1, :] != 0
        value = v_ref[:, head_columns(j)]
        grad = g_ref[:, head_columns(j)]
        raw = qk_ref[:, head_columns(j)].astype(F32)
        factor, normed = normalise(raw)
        second = pick(upper, grad, value)
        first = pick(upper, value, grad)
        their_normed = z_ref[j, :, 0:PAIRS].reshape(TILE, HEAD_DIM)
        their_second = z_ref[j, :, PAIRS : 2 * PAIRS].reshape(TILE, HEAD_DIM)
        stats = z_ref[j, :, 2 * PAIRS].reshape(2 * SLICES, TILE).astype(F32)
        their_total = stats[0:1] + stats[1:2]
        their_moment = stats[2:3] + stats[3:4]
        keys = jnp.concatenate([normed, their_normed], axis=0)
        others = jnp.concatenate([first, their_second], axis=0)
        yield
        scores = [dot_nt(normed, normed), dot_nt(normed, their_normed)]
        weights = jnp.exp2(jnp.concatenate(scores, axis=1) * SCALE_LOG2)
        grad_probs = dot_nt(second, others)
        yield
        inside = jnp.where(upper, ahead, -ahead) >= 0
        own_w = jnp.where(inside, weights[:, :TILE], 0.0)
        cross_w = weights[:, TILE:]
        own_g = grad_probs[:, :TILE]
        cross_g = grad_probs[:, TILE:]
        inv_row = 1.0 / jnp.sum(own_w + cross_w, axis=1, keepdims=True)
        own_inv = 1.0 / jnp.sum(own_w, axis=0, keepdims=True)
        cross_inv = 1.0 / (their_total + jnp.sum(cross_w, axis=0, keepdims=True))
        yield
        own_p = (own_w * jnp.where(upper, inv_row, own_inv)).astype(BF16)
        cross_p = (cross_w * jnp.where(upper, inv_row, cross_inv)).astype(BF16)
        own_f = own_p.astype(F32)
        cross_f = cross_p.astype(F32)
        own_t = own_f * own_g
        cross_t = cross_f * cross_g
        yield
        row_sum = jnp.sum(own_t + cross_t, axis=1, keepdims=True)
        own_sum = jnp.sum(own_t, axis=0, keepdims=True)
        cross_sum = their_moment * cross_inv + jnp.sum(cross_t, axis=0, keepdims=True)
        yield
        own_s = own_f * (own_g - jnp.where(upper, row_sum, own_sum))
        cross_s = cross_f * (cross_g - jnp.where(upper, row_sum, cross_sum))
        own_s = own_s.astype(BF16)
        scores = jnp.concatenate([own_s, cross_s.astype(BF16)], axis=1)
        along = dot_nn(jnp.concatenate([own_p, cross_p], axis=1), others)
        across = dot_tn(own_p, second)
        grad_normed = dot_nn(scores, keys) + dot_tn(own_s, normed)
        yield
        out_ref[:, head_columns(j)] = jnp.where(upper, along, across).astype(BF16)
        grads_ref[1, :, head_columns(j)] = jnp.where(upper, across, along).astype(BF16)
        grad_normed = (grad_normed * SCALE).astype(BF16).astype(F32)
        inner = jnp.mean(raw * grad_normed, axis=-1, keepdims=True)
        grad_input = factor * grad_normed - raw * (factor**3 * inner)
        grads_ref[0, :, head_columns(j)] = grad_input.astype(BF16)

    for start in range(0, HEADS, GROUP):
        in_step([head(start + j) for j in range(GROUP)])


def finish(upper, qk, value, grad, z):
    shape = jax.ShapeDtypeStruct((TILE, HEADS * HEAD_DIM), BF16)
    whole = pl.BlockSpec(memory_space=pltpu.VMEM)
    return pl.pallas_call(
        finish_kernel,
        out_shape=(shape, jax.ShapeDtypeStruct((2, *shape.shape), shape.dtype)),
        in_specs=[whole] * 5,
        out_specs=(whole, whole),
        compiler_params=pltpu.CompilerParams(vmem_limit_bytes=VMEM_LIMIT),
        name="finish",
    )(upper, qk, value, grad, z)


def deliver_kernel(x_ref, o_hbm, sem):
    copy = pltpu.make_async_copy(x_ref, o_hbm, sem)
    copy.start()
    copy.wait()


def deliver(x):
    return pl.pallas_call(
        deliver_kernel,
        out_shape=pltpu.HBM(x.shape, x.dtype),
        in_specs=[pl.BlockSpec(memory_space=pltpu.VMEM)],
        out_specs=pl.BlockSpec(memory_space=pltpu.HBM),
        scratch_shapes=[pltpu.SemaphoreType.DMA],
        compiler_params=pltpu.CompilerParams(vmem_limit_bytes=VMEM_LIMIT),
        cost_estimate=pl.CostEstimate(
            flops=0, bytes_accessed=2 * x.size * x.dtype.itemsize, transcendentals=0
        ),
        name="deliver",
    )(x)


def deliver_pair_kernel(x_ref, a_hbm, b_hbm, sems):
    copies = [
        pltpu.make_async_copy(x_ref.at[i], o_hbm, sems.at[i])
        for i, o_hbm in enumerate((a_hbm, b_hbm))
    ]
    for copy in copies:
        copy.start()
    for copy in copies:
        copy.wait()


def deliver_pair(x):
    hbm = pl.BlockSpec(memory_space=pltpu.HBM)
    return pl.pallas_call(
        deliver_pair_kernel,
        out_shape=(pltpu.HBM(x.shape[1:], x.dtype),) * 2,
        in_specs=[pl.BlockSpec(memory_space=pltpu.VMEM)],
        out_specs=(hbm, hbm),
        scratch_shapes=[pltpu.SemaphoreType.DMA((2,))],
        compiler_params=pltpu.CompilerParams(vmem_limit_bytes=VMEM_LIMIT),
        name="deliver_pair",
    )(x)


def exchange(x):
    return lax.all_to_all(x, "seq", split_axis=0, concat_axis=0, tiled=True)


def local(query_key, payload_matrix, out_grad, route_assignment):
    route = route_assignment[0]
    rows = (query_key[0], payload_matrix[0], out_grad[0])
    packed, upper, partner = pack(route.T, *rows)
    slices = exchange(packed.reshape(TILES, MSG, 2, HEAD_DIM))
    theirs = exchange(swap(partner, slices)).reshape(HEADS, SLICES, MSG, 2, HEAD_DIM)
    out, grads = finish(upper, *rows, theirs)
    grads = lax.ppermute(grads, "pipe", [(0, 1), (1, 0)])
    out, (grad_qk, grad_v) = deliver(out), deliver_pair(grads)
    return (out[None], grad_qk[None], grad_v[None])


def solution(mesh):
    rows = P("pipe", "seq", None)
    return jax.shard_map(
        local,
        mesh=mesh,
        in_specs=(rows, rows, rows, P("pipe", None, None)),
        out_specs=(rows, rows, rows),
        check_vma=False,
    )
```
